256 devices in a mesh: wide: 64 (over y, z, core), narrow: 4 (over x).
Axes of the slice: x: 4, y: 4, z: 8, core: 2. Of those that a mesh axis runs over, the one named last changes fastest.
Arguments:
- left_edge: bfloat16 [448, 49, 448], P('wide', None, 'narrow'), may hold values from -40 to 40
- corner: bfloat16 [448, 448], P('narrow'), may hold values from -0.25 to 0.25
- right_edge: bfloat16 [448, 49, 448], P('wide', None, 'narrow'), may hold values from -0.25 to 0.25
- single_layer: bfloat16 [2, 2401], replicated, may hold values from -0.71875 to 0.71875
- warm_basis: bfloat16 [49, 448, 448], P(None, 'narrow', 'wide'), may hold values from -0.0390625 to 0.0390625
Outputs:
- new_basis: float32 [448, 49, 448], P('wide', None, 'narrow')
- r_factor: float32 [448, 448], replicated
The draws below stay inside these ranges and needn't reach their ends.
All inputs are finite; a program needn't handle non-finite values.
Results may differ from the reference program's by a relative error of at most 0.014.
Values may be sent and summed in bfloat16 or wider, within the bound.
A program may use at most 128 MiB of HBM per device.

```python
import math
import jax
import jax.numpy as jnp
from jax import lax

BOND = 7
PHYS = 2
CHI = 448
DD = 49
N_WIDE = 64


def draw_left_edge(key, part):
    first, second = jax.random.split(key, 2)
    scales = jnp.exp(jax.random.uniform(first, (CHI, 1, 1), jnp.float32) * math.log(10.0))
    base = jnp.clip(jax.random.normal(second, (CHI, DD, CHI), jnp.float32), -4.0, 4.0)
    return (base * scales).astype(jnp.bfloat16)


def block_levels(own_key, dims, shards, least, top_value):
    loudness = 1.0
    for axis_at, parts in shards:
        heights = jax.random.uniform(jax.random.fold_in(jax.random.fold_in(own_key, 6), axis_at), (parts,), jnp.float32, least / len(shards), top_value / len(shards))
        loudness = loudness * jnp.repeat(jnp.exp(heights), dims[axis_at] // parts).reshape((-1,) + (1,) * (len(dims) - 1 - axis_at))
    return loudness


def centred(key, extent, deviation, most, cuts=(), kind=jnp.bfloat16):
    array = deviation * jax.random.normal(key, extent, jnp.float32)
    if cuts:
        array = array * block_levels(key, extent, cuts, -0.22, 0.18)
    return jnp.clip(array, -most, most).astype(kind)


def setup_inputs(seed: int = 0) -> dict:
    key_list = jax.random.split(jax.random.key(seed), 6)
    left_edge = draw_left_edge(jax.random.fold_in(key_list[5], 71), 0)
    corner = centred(key_list[1], (CHI, CHI), CHI ** -0.5, 0.25, ((0, 4),))
    right_edge = centred(key_list[2], (CHI, DD, CHI), CHI ** -0.5, 0.25, ((0, 64), (2, 4)))
    single_layer = centred(key_list[3], (PHYS, DD * DD), 0.12, 0.71875)
    warm_basis = centred(key_list[4], (DD, CHI, CHI), (DD * CHI) ** -0.5, 0.0390625, ((1, 4), (2, 64)))
    return dict(left_edge=left_edge, corner=corner, right_edge=right_edge, single_layer=single_layer, warm_basis=warm_basis)


def reference(left_edge, corner, right_edge, single_layer, warm_basis):
    layer = single_layer.astype(jnp.float32).reshape(PHYS, BOND, BOND, BOND, BOND)
    half_left = jnp.dot(left_edge.reshape(CHI * DD, CHI).astype(jnp.float32), corner.astype(jnp.float32), preferred_element_type=jnp.float32).astype(jnp.bfloat16)
    block = CHI // N_WIDE
    side_matrix = right_edge.reshape(CHI, DD * CHI)
    basis_matrix = warm_basis.reshape(DD * CHI, CHI)

    def one_block(rows_block):
        strip = jnp.dot(rows_block.reshape(block * DD, CHI).astype(jnp.float32), side_matrix.astype(jnp.float32), preferred_element_type=jnp.float32)
        strip = strip.astype(jnp.bfloat16).astype(jnp.float32).reshape(block, BOND, BOND, BOND, BOND, CHI)
        ket_layer = jnp.einsum('iuvlmj,suldr->ivmsdrj', strip, layer)
        enlarged = jnp.einsum('ivmsdrj,svmew->iderwj', ket_layer, layer)
        enlarged = enlarged.astype(jnp.bfloat16).reshape(block * DD, DD * CHI)
        return jnp.dot(enlarged.astype(jnp.float32), basis_matrix.astype(jnp.float32), preferred_element_type=jnp.float32)
    projected = lax.map(one_block, half_left.reshape(CHI // block, block, DD, CHI)).reshape(CHI * DD, CHI)
    gram = jnp.dot(projected.T.astype(jnp.float32), projected.astype(jnp.float32), precision=lax.Precision.HIGHEST, preferred_element_type=jnp.float32) / (CHI * DD)
    lower = jnp.linalg.cholesky(gram)
    solved = lax.linalg.triangular_solve(lower, projected.T, left_side=True, lower=True)
    return (solved.T.reshape(CHI, DD, CHI), lower.T)
```

```python
import functools

import jax
import jax.numpy as jnp
from jax import lax
from jax.experimental import pallas as pl
from jax.experimental.pallas import tpu as pltpu
from jax.sharding import PartitionSpec as P

BOND = 7
BLOCK = 64
SLOT = 16
HALF = 3200
A_LANES = 1280
ROWS = 400
HI = lax.Precision.HIGHEST
MESH = pl.DeviceIdType.MESH
MIB = 1 << 20


def place():
    wide = lax.axis_index("wide")
    core = lax.rem(wide, 2)
    z = lax.rem(lax.div(wide, 2), 8)
    y = lax.div(wide, 16)
    return y, z, core, lax.axis_index("narrow")


def wide_of(y, z, core):
    return (y * 8 + z) * 2 + core


def greet(peers):
    barrier = pltpu.get_barrier_semaphore()
    for peer in peers:
        pl.semaphore_signal(barrier, inc=1, device_id=peer, device_id_type=MESH)
    pl.semaphore_wait(barrier, len(peers))


def gather_kernel(right, warm, left, corner, right_all, warm_all, left_all, corner_all,
                  paired, merged, pair_s, pair_r, own_s, ring_r, near_s, far_s, yl_s, ys_s, first_s,
                  part_s, part_r, x_s, x_r):
    y, z, core, x = place()
    zdir = 1 - 2 * core

    def zmove(k):
        return lax.rem(z + 8 + k * zdir, 8)

    def ymove(k):
        return lax.rem(y + 4 + k * zdir, 4)

    def at(yy, zz, cc=None):
        return (wide_of(yy, zz, core if cc is None else cc), x)

    partner = at(y, z, 1 - core)
    peers = [partner, at(y, zmove(1)), at(y, zmove(-1)), at(ymove(1), z), at(ymove(2), z), at(ymove(3), z)]
    peers += [(wide_of(y, z, core), lax.rem(x + d, 4)) for d in (1, 2, 3)]
    greet(peers)

    pending = []

    def push(src, dst, ss, rs, device):
        c = pltpu.make_async_remote_copy(src_ref=src, dst_ref=dst, send_sem=ss, recv_sem=rs,
                                         device_id=device, device_id_type=MESH)
        c.start()
        pending.append(c)

    arrays = ((right, right_all), (warm, warm_all))
    pairs = []
    for g, (src, _) in enumerate(arrays):
        c = pltpu.make_async_remote_copy(src_ref=src.at[1 - core], dst_ref=paired.at[g], send_sem=pair_s.at[g],
                                         recv_sem=pair_r.at[g], device_id=partner, device_id_type=MESH)
        c.start()
        pairs.append(c)
    xcopies = []
    for src, dst, k in ((left, left_all, 0), (corner, corner_all, 1)):
        for d in (1, 2, 3):
            c = pltpu.make_async_remote_copy(
                src_ref=src, dst_ref=dst.at[x], send_sem=x_s.at[k, d - 1], recv_sem=x_r.at[k, d - 1],
                device_id=(wide_of(y, z, core), lax.rem(x + d, 4)), device_id_type=MESH)
            c.start()
            xcopies.append(c)
    own_x = []
    for src, dst, k in ((left, left_all, 0), (corner, corner_all, 1)):
        c = pltpu.make_async_copy(src, dst.at[x], own_s.at[2 + k])
        c.start()
        own_x.append(c)

    bounds = ((0, A_LANES), (A_LANES, HALF))

    def view(g, half, part, yy, zz):
        lo, hi = bounds[part]
        rows = pl.ds(pl.multiple_of((yy * 8 + zz) * SLOT, SLOT), SLOT)
        return arrays[g][1].at[half, rows, lo:hi]

    def slot(yy, zz):
        return yy * 8 + zz

    def send(g, part, yy, zz, sem, device, src=None):
        v = view(g, core, part, yy, zz)
        push(v if src is None else src, v, sem.at[g, part, slot(yy, zz)], ring_r.at[g, part, slot(yy, zz)], device)

    def forward_partner(g, part, yy, zz, src=None):
        v = view(g, core, part, yy, zz)
        push(v if src is None else src, v, part_s.at[g, part, slot(yy, zz)], part_r.at[g, part, slot(yy, zz)], partner)

    def arrived(g, part, yy, zz):
        v = view(g, core, part, yy, zz)
        pltpu.make_async_copy(v, v, ring_r.at[g, part, slot(yy, zz)]).wait()

    own_copies = []
    znext, zprev = at(y, zmove(1)), at(y, zmove(-1))
    ynext, yprev = at(ymove(1), z), at(ymove(-1), z)

    def begin(g):
        pairs[g].wait()
        merged[g] = paired[g] + arrays[g][0][core]
        c = pltpu.make_async_copy(
            merged.at[g], arrays[g][1].at[core, pl.ds(pl.multiple_of((y * 8 + z) * SLOT, SLOT), SLOT), :], own_s.at[g])
        c.start()
        own_copies.append(c)
        a, b = merged.at[g, :, 0:A_LANES], merged.at[g, :, A_LANES:HALF]
        va = view(g, core, 0, y, z)
        for d in (1, 2, 3):
            push(a, va, first_s.at[g, d - 1], ring_r.at[g, 0, slot(y, z)], at(ymove(d), z))
        send(g, 1, y, z, near_s, znext, b)
        send(g, 1, y, z, far_s, zprev, b)
        send(g, 0, y, z, near_s, znext, a)
        send(g, 0, y, z, far_s, zprev, a)
        send(g, 1, y, z, yl_s, ynext, b)
        send(g, 1, y, z, ys_s, yprev, b)
        forward_partner(g, 0, y, z, a)
        forward_partner(g, 1, y, z, b)

    def column(g):
        for d in (1, 2, 3):
            yy = ymove(d)
            arrived(g, 0, yy, z)
            send(g, 0, yy, z, near_s, znext)
            send(g, 0, yy, z, far_s, zprev)
            forward_partner(g, 0, yy, z)

    def b_ring(g, s, way):
        zz = zmove(-s) if way > 0 else zmove(s)
        arrived(g, 1, y, zz)
        if way > 0 and s < 4:
            send(g, 1, y, zz, near_s, znext)
        if way < 0 and s < 3:
            send(g, 1, y, zz, far_s, zprev)
        send(g, 1, y, zz, yl_s, ynext)
        send(g, 1, y, zz, ys_s, yprev)
        forward_partner(g, 1, y, zz)

    def a_ring(g, s, way, d):
        zz = zmove(-s) if way > 0 else zmove(s)
        yy = ymove(d)
        arrived(g, 0, yy, zz)
        if way > 0 and s < 4:
            send(g, 0, yy, zz, near_s, znext)
        if way < 0 and s < 3:
            send(g, 0, yy, zz, far_s, zprev)
        forward_partner(g, 0, yy, zz)

    def y_pass(g, zz):
        arrived(g, 1, ymove(-1), zz)
        send(g, 1, ymove(-1), zz, yl_s, ynext)
        forward_partner(g, 1, ymove(-1), zz)
        arrived(g, 1, ymove(1), zz)
        forward_partner(g, 1, ymove(1), zz)

    def y_last(g, zz):
        arrived(g, 1, ymove(2), zz)
        forward_partner(g, 1, ymove(2), zz)

    def ring(g):
        y_pass(g, z)
        for s in (1, 2, 3, 4):
            for way in (1, -1):
                if way < 0 and s == 4:
                    continue
                b_ring(g, s, way)
                for d in range(4):
                    a_ring(g, s, way, d)
            if s > 1:
                y_pass(g, zmove(-(s - 1)))
                y_pass(g, zmove(s - 1))

    def finish(g):
        y_pass(g, zmove(-4))
        for k in range(8):
            y_last(g, zmove(k))

    for g in (0, 1):
        begin(g)
    for g in (0, 1):
        column(g)
    for g in (0, 1):
        ring(g)
    for g in (0, 1):
        finish(g)
    for g in (0, 1):
        for part in (0, 1):
            for s in range(32):
                v = view(g, 1 - core, part, s // 8, s % 8)
                pltpu.make_async_copy(v, v, part_r.at[g, part, s]).wait()
    for c in pending:
        c.wait_send()
    for c in xcopies:
        c.wait()
    for c in own_copies + own_x:
        c.wait()


def gathers(right, warm, left, corner):
    dma = pltpu.SemaphoreType.DMA
    any_ = pl.BlockSpec(memory_space=pl.ANY)
    vm = pl.BlockSpec(memory_space=pltpu.VMEM)
    return pl.pallas_call(
        gather_kernel,
        out_shape=[
            jax.ShapeDtypeStruct((2, 32 * SLOT, HALF), jnp.bfloat16),
            jax.ShapeDtypeStruct((2, 32 * SLOT, HALF), jnp.bfloat16),
            jax.ShapeDtypeStruct((4, ROWS, 128), jnp.bfloat16),
            jax.ShapeDtypeStruct((4, 128, 512), jnp.bfloat16),
        ],
        in_specs=[vm] * 4,
        out_specs=[any_] * 4,
        scratch_shapes=[
            pltpu.VMEM((2, SLOT, HALF), jnp.bfloat16),
            pltpu.VMEM((2, SLOT, HALF), jnp.bfloat16),
            dma((2,)), dma((2,)), dma((4,)), dma((2, 2, 32)), dma((2, 2, 32)), dma((2, 2, 32)),
            dma((2, 2, 32)), dma((2, 2, 32)), dma((2, 3)), dma((2, 2, 32)), dma((2, 2, 32)), dma((2, 3)), dma((2, 3)),
        ],
        compiler_params=pltpu.CompilerParams(collective_id=1, has_side_effects=True, vmem_limit_bytes=48 * MIB),
        name="gathers",
    )(right, warm, left, corner)


def contract_kernel(right, warm, left, corner, ket, bra, pick, out, half, strip, layered, enlarged, total):
    acc = jnp.zeros((ROWS, 512), jnp.float32)
    for n in range(4):
        acc += jnp.dot(left[n], corner[n], preferred_element_type=jnp.float32)
    half[...] = acc.astype(jnp.bfloat16)

    for h in range(2):
        @pl.loop(0, 5)
        def _(chunk):
            cols = pl.ds(pl.multiple_of(chunk * 640, 640), 640)
            res = jnp.dot(half[...], right[h, :, cols], preferred_element_type=jnp.float32)
            for j in range(5):
                rows = pl.ds(pl.multiple_of((h * 25 + chunk * 5 + j) * 8, 8), 8)
                strip[:, rows, :] = res[:, j * 128:(j + 1) * 128].reshape(50, 8, 128)

    @pl.loop(0, 25)
    def _(t):
        x = jnp.concatenate([strip[2 * t].astype(jnp.bfloat16), strip[2 * t + 1].astype(jnp.bfloat16)], axis=1)
        res = jnp.dot(ket[...], x, preferred_element_type=jnp.float32).astype(jnp.bfloat16)
        for j in range(2):
            rows = pl.ds(pl.multiple_of((2 * t + j) * 16, 16), 16)
            layered[:, rows, :] = res[:, j * 128:(j + 1) * 128].reshape(49, 16, 128)

    enlarged[49] = jnp.zeros((ROWS, 128), jnp.float32)

    @pl.loop(0, 50)
    def _(b):
        enlarged[b, 392:400, :] = jnp.zeros((8, 128), jnp.float32)

    @pl.loop(0, 49)
    def _(dr):
        d, r = lax.div(dr, 7), lax.rem(dr, 7)
        x = jnp.concatenate([layered[dr, i * 112:(i + 1) * 112, :] for i in range(7)], axis=1)
        res = jnp.dot(bra[...], x, preferred_element_type=jnp.float32)
        for i in range(7):
            rows = pl.ds(pl.multiple_of((i * 7 + d) * 8, 8), 8)
            for s in range(7):
                enlarged[r * 7 + s, rows, :] = res[s * 8:(s + 1) * 8, i * 128:(i + 1) * 128]

    total[...] = jnp.zeros_like(total)
    for h in range(2):
        @pl.loop(0, 5)
        def _(chunk):
            cols = pl.ds(pl.multiple_of(chunk * 640, 640), 640)
            x = jnp.concatenate(
                [enlarged[h * 25 + chunk * 5 + j].astype(jnp.bfloat16) for j in range(5)], axis=1)
            total[...] += lax.dot_general(x, warm[h, :, cols], (((1,), (1,)), ((), ())),
                                          preferred_element_type=jnp.float32)
    res = jnp.dot(total[...].astype(jnp.bfloat16), pick[...], preferred_element_type=jnp.float32)
    for n in range(4):
        out[n] = res[:, n * 128:(n + 1) * 128].astype(jnp.bfloat16)


def contract(right, warm, left, corner, ket, bra, pick):
    vm = pl.BlockSpec(memory_space=pltpu.VMEM)
    return pl.pallas_call(
        contract_kernel,
        out_shape=jax.ShapeDtypeStruct((4, ROWS, 128), jnp.bfloat16),
        in_specs=[vm] * 7,
        out_specs=vm,
        scratch_shapes=[
            pltpu.VMEM((ROWS, 512), jnp.bfloat16),
            pltpu.VMEM((50, ROWS, 128), jnp.float32),
            pltpu.VMEM((49, 800, 128), jnp.bfloat16),
            pltpu.VMEM((50, ROWS, 128), jnp.float32),
            pltpu.VMEM((ROWS, 512), jnp.float32),
        ],
        compiler_params=pltpu.CompilerParams(vmem_limit_bytes=60 * MIB),
        name="contract",
    )(right, warm, left, corner, ket, bra, pick)


def sums_kernel(part, proj, gram, got, slab, got1, piece, got2, n_s, n_r, p_s, p_r, a_s, a_r, b_s, b_r,
                c_s, c_r, d_s, d_r, e_s, e_r, f_s, f_r):
    y, z, core, x = place()
    others = [(lax.rem(y + k // 2, 4), lax.rem(core + k % 2, 2)) for k in range(1, 8)]
    xs = [lax.rem(x + d, 4) for d in (1, 2, 3)]
    zs = [lax.rem(z + d, 8) for d in range(1, 8)]
    me = wide_of(y, z, core)
    greet([(me, xx) for xx in xs] + [(wide_of(yy, z, cc), x) for yy, cc in others]
          + [(wide_of(y, zz, core), x) for zz in zs])

    def start(src, dst, ss, rs, device):
        c = pltpu.make_async_remote_copy(src_ref=src, dst_ref=dst, send_sem=ss, recv_sem=rs,
                                         device_id=device, device_id_type=MESH)
        c.start()
        return c

    c1 = [start(part.at[xs[d]], got.at[d], n_s.at[d], n_r.at[d], (me, xs[d])) for d in range(3)]
    acc = part[x].astype(jnp.float32)
    for d in range(3):
        c1[d].wait_recv()
        acc += got[d].astype(jnp.float32)
    proj[x] = acc.astype(jnp.bfloat16)
    c2 = [start(proj.at[x], proj.at[x], p_s.at[d], p_r.at[d], (me, xs[d])) for d in range(3)]
    own = acc.astype(jnp.bfloat16)
    tn = (((0,), (0,)), ((), ()))
    scale = 1.0 / (448 * 49)

    def product(n):
        slab[pl.ds(pl.multiple_of(n * 128, 128), 128), :] = lax.dot_general(
            proj[n], own, tn, preferred_element_type=jnp.float32) * scale

    product(x)
    for d in (0, 2, 1):
        c2[d].wait_recv()
        product(lax.rem(x + 3 - d, 4))

    def rows(k, size):
        return pl.ds(pl.multiple_of(k * size, size), size)

    mine = y * 2 + core
    c3 = [start(slab.at[rows(yy * 2 + cc, 64)], got1.at[k], a_s.at[k], a_r.at[k], (wide_of(yy, z, cc), x))
          for k, (yy, cc) in enumerate(others)]
    acc = slab[rows(mine, 64), :]
    for k in range(7):
        c3[k].wait_recv()
        acc += got1[k]
    piece[...] = acc
    c4 = [start(piece.at[rows(zz, 8)], got2.at[k], b_s.at[k], b_r.at[k], (wide_of(y, zz, core), x))
          for k, zz in enumerate(zs)]
    acc = piece[rows(z, 8), :]
    for k in range(7):
        c4[k].wait_recv()
        acc += got2[k]
    spot = gram.at[x, y, core, rows(z, 8)]
    gram[x, y, core, rows(z, 8), :] = acc
    c5 = [start(spot, spot, c_s.at[k], c_r.at[k], (wide_of(y, zz, core), x)) for k, zz in enumerate(zs)]
    for c in c5:
        c.wait_recv()
    spot = gram.at[x, y, core]
    c6 = [start(spot, spot, d_s.at[d], d_r.at[d], (me, xs[d])) for d in range(3)]
    for c in c6:
        c.wait_recv()
    spot = gram.at[:, y, core]
    c7 = [start(spot, spot, e_s.at[d - 1], e_r.at[d - 1], (wide_of(lax.rem(y + d, 4), z, core), x)) for d in (1, 2, 3)]
    other = (wide_of(y, z, 1 - core), x)
    c8 = [start(spot, spot, f_s.at[0], f_r.at[0], other)]
    for d in (3, 1, 2):
        c7[d - 1].wait_recv()
        spot = gram.at[:, lax.rem(y + 4 - d, 4), core]
        c8.append(start(spot, spot, f_s.at[d], f_r.at[d], other))
    for c in c8:
        c.wait()
    for c in c1 + c2 + c3 + c4 + c5 + c6 + c7:
        c.wait_send()


def sums(part):
    dma = pltpu.SemaphoreType.DMA
    vm = pl.BlockSpec(memory_space=pltpu.VMEM)
    return pl.pallas_call(
        sums_kernel,
        out_shape=[
            jax.ShapeDtypeStruct((4, ROWS, 128), jnp.bfloat16),
            jax.ShapeDtypeStruct((4, 4, 2, 64, 128), jnp.float32),
        ],
        in_specs=[vm],
        out_specs=[vm, vm],
        scratch_shapes=[
            pltpu.VMEM((3, ROWS, 128), jnp.bfloat16),
            pltpu.VMEM((512, 128), jnp.float32),
            pltpu.VMEM((7, 64, 128), jnp.float32),
            pltpu.VMEM((64, 128), jnp.float32),
            pltpu.VMEM((7, 8, 128), jnp.float32),
            dma((3,)), dma((3,)), dma((3,)), dma((3,)), dma((7,)), dma((7,)), dma((7,)), dma((7,)),
            dma((7,)), dma((7,)), dma((3,)), dma((3,)), dma((3,)), dma((3,)), dma((4,)), dma((4,)),
        ],
        compiler_params=pltpu.CompilerParams(collective_id=2, has_side_effects=True, vmem_limit_bytes=32 * MIB),
        name="sums",
    )(part)


def eliminate(diag):
    n = BLOCK
    row_id = lax.broadcasted_iota(jnp.int32, (n, n), 0)
    col_id = lax.broadcasted_iota(jnp.int32, (n, n), 1)
    eye = jnp.where(row_id == col_id, 1.0, 0.0).astype(jnp.float32)
    wide = jnp.concatenate([diag, eye], axis=1)
    groups = [wide[8 * g:8 * g + 8] for g in range(n // 8)]
    sub = lax.broadcasted_iota(jnp.int32, (8, 2 * n), 0)
    for k in range(n):
        g, t = divmod(k, 8)
        pivot = groups[g][t:t + 1, :]
        scaled = pivot * (1.0 / pivot[:, k:k + 1])
        for h in range(g, n // 8):
            if h == g and t == 7:
                continue
            update = groups[h][:, k:k + 1] * scaled
            if h == g:
                update = jnp.where(sub > t, update, 0.0)
            groups[h] = groups[h] - update
    wide = jnp.concatenate(groups, axis=0)
    upper, lower = wide[:, :n], wide[:, n:]
    d = jnp.sum(upper * eye, axis=1, keepdims=True)
    root = lax.rsqrt(d)
    root = root * (1.5 - 0.5 * d * root * root)
    return jnp.where(row_id <= col_id, upper * root, 0.0), jnp.where(row_id >= col_id, lower * root, 0.0)


def factor_kernel(gram, proj, r_ref, out, work):
    n = 448
    x = lax.axis_index("narrow")
    for a in range(4):
        for b in range(4):
            work[a * 112:(a + 1) * 112, b * 112:(b + 1) * 112] = gram[b, a * 128:a * 128 + 112, 0:112]
    r_ref[...] = jnp.zeros_like(r_ref)
    col = lax.broadcasted_iota(jnp.int32, (BLOCK, n), 1)
    row = lax.broadcasted_iota(jnp.int32, (BLOCK, n), 0)
    for b in range(n // BLOCK):
        lo, hi = b * BLOCK, (b + 1) * BLOCK
        r, inverse = eliminate(work[lo:hi, lo:hi])
        inside = (col >= lo) & (col < hi)
        src = jnp.where(inside, jnp.where(col - lo == row, 1.0, 0.0), work[lo:hi, :])
        full = jnp.dot(inverse, src, precision=HI, preferred_element_type=jnp.float32)
        work[lo:hi, :] = jnp.where(col < hi, full, 0.0)
        rest = jnp.where(col >= hi, full, 0.0)
        r_ref[lo:hi, :] = rest
        r_ref[lo:hi, lo:hi] = r
        if hi < n:
            at = lax.broadcasted_iota(jnp.int32, (n - hi, n), 1)
            old = jnp.where((at >= lo) & (at < hi), 0.0, work[hi:, :])
            work[hi:, :] = old - lax.dot_general(rest[:, hi:], full, (((0,), (0,)), ((), ())), precision=HI,
                                                 preferred_element_type=jnp.float32)
    own = work[pl.ds(pl.multiple_of(x * 112, 8), 112), :]
    nt = (((1,), (1,)), ((), ()))
    acc = jnp.zeros((ROWS, 112), jnp.float32)
    for b in range(4):
        acc += lax.dot_general(proj[b][:, 0:112].astype(jnp.float32), own[:, b * 112:(b + 1) * 112], nt, precision=HI,
                               preferred_element_type=jnp.float32)
    out[...] = acc


def factor(gram, proj):
    vm = pl.BlockSpec(memory_space=pltpu.VMEM)
    return pl.pallas_call(
        factor_kernel,
        out_shape=[jax.ShapeDtypeStruct((448, 448), jnp.float32), jax.ShapeDtypeStruct((ROWS, 112), jnp.float32)],
        in_specs=[vm, vm],
        out_specs=[vm, vm],
        scratch_shapes=[pltpu.VMEM((448, 448), jnp.float32)],
        compiler_params=pltpu.CompilerParams(vmem_limit_bytes=40 * MIB),
        name="factor",
    )(gram, proj)


def shard_rows(block, core):
    rows = jnp.pad(block, ((0, 0), (0, 1), (0, 16))).reshape(7, 2, HALF).transpose(1, 0, 2)
    return jnp.where(core == 0, jnp.pad(rows, ((0, 0), (0, 9), (0, 0))), jnp.pad(rows, ((0, 0), (7, 2), (0, 0))))


def layers(single_layer):
    layer = single_layer.reshape(2, BOND, BOND, BOND, BOND)
    eye = jnp.eye(BOND, dtype=layer.dtype)
    ket = jnp.einsum("suldr,mn->drsmlnu", layer, eye)
    ket = jnp.pad(ket.reshape(49, 14, 49, 7), ((0, 0), (0, 2), (0, 1), (0, 1))).reshape(784, ROWS)
    bra = layer.transpose(4, 3, 1, 0, 2).reshape(7, 7, 7, 14)
    bra = jnp.pad(bra, ((0, 0), (0, 1), (0, 0), (0, 2))).reshape(56, 112)
    return ket, bra


def picker():
    at = lax.broadcasted_iota(jnp.int32, (512, 512), 0)
    to = lax.broadcasted_iota(jnp.int32, (512, 512), 1)
    held = jnp.where(at % 16 < 14, at // 16 * 14 + at % 16, -1)
    wanted = jnp.where(to % 128 < 112, to // 128 * 112 + to % 128, -2)
    return (held == wanted).astype(jnp.bfloat16)


def on_device(left_edge, corner, right_edge, single_layer, warm_basis):
    core = lax.axis_index("wide") % 2
    right = shard_rows(right_edge, core)
    warm = shard_rows(warm_basis.transpose(2, 0, 1), core)
    left = left_edge.reshape(7, 7, 7, 112).transpose(0, 2, 1, 3)
    left = jnp.pad(left, ((0, 0), (0, 0), (0, 1), (0, 16))).reshape(392, 128)
    left = jnp.pad(left, ((0, 8), (0, 0)))
    corner = jnp.pad(corner.reshape(112, 32, 14), ((0, 16), (0, 0), (0, 2))).reshape(128, 512)
    ket, bra = layers(single_layer)
    right, warm, left, corner = gathers(right, warm, left, corner)
    part = contract(right, warm, left, corner, ket, bra, picker())
    proj, gram = sums(part)
    r_factor, rows = factor(gram.reshape(4, 512, 128), proj)
    new_basis = rows[:392].reshape(7, 7, 8, 112)[:, :, :7].reshape(7, 49, 112)
    return new_basis, r_factor


def solution(mesh):
    placed = (
        P("wide", None, "narrow"),
        P("narrow", None),
        P("wide", None, "narrow"),
        P(),
        P(None, "narrow", "wide"),
    )
    return jax.shard_map(
        on_device,
        mesh=mesh,
        in_specs=placed,
        out_specs=(P("wide", None, "narrow"), P()),
        check_vma=False,
    )
```

```python
import functools

import jax
import jax.numpy as jnp
from jax import lax
from jax.experimental import pallas as pl
from jax.experimental.pallas import tpu as pltpu
from jax.sharding import PartitionSpec as P

BOND = 7
BLOCK = 64
SLOT = 16
HALF = 3200
A_LANES = 1280
ROWS = 400
HI = lax.Precision.HIGHEST
MESH = pl.DeviceIdType.MESH
MIB = 1 << 20


def place():
    wide = lax.axis_index("wide")
    core = lax.rem(wide, 2)
    z = lax.rem(lax.div(wide, 2), 8)
    y = lax.div(wide, 16)
    return y, z, core, lax.axis_index("narrow")


def wide_of(y, z, core):
    return (y * 8 + z) * 2 + core


def greet(peers):
    barrier = pltpu.get_barrier_semaphore()
    for peer in peers:
        pl.semaphore_signal(barrier, inc=1, device_id=peer, device_id_type=MESH)
    pl.semaphore_wait(barrier, len(peers))


def gather_kernel(right, warm, left, corner, layer, out,
                  right_all, warm_all, left_all, corner_all, half, strip, layered, total, ket, bra,
                  paired, merged, pair_s, pair_r, own_s, ring_r, near_s, far_s, yl_s, ys_s, first_s,
                  part_s, part_r, x_s, x_r):
    y, z, core, x = place()
    zdir = 1 - 2 * core

    def zmove(k):
        return lax.rem(z + 8 + k * zdir, 8)

    def ymove(k):
        return lax.rem(y + 4 + k * zdir, 4)

    def at(yy, zz, cc=None):
        return (wide_of(yy, zz, core if cc is None else cc), x)

    partner = at(y, z, 1 - core)
    peers = [partner, at(y, zmove(1)), at(y, zmove(-1)), at(ymove(1), z), at(ymove(2), z), at(ymove(3), z)]
    peers += [(wide_of(y, z, core), lax.rem(x + d, 4)) for d in (1, 2, 3)]
    greet(peers)

    pending = []

    def push(src, dst, ss, rs, device):
        c = pltpu.make_async_remote_copy(src_ref=src, dst_ref=dst, send_sem=ss, recv_sem=rs,
                                         device_id=device, device_id_type=MESH)
        c.start()
        pending.append(c)

    arrays = ((right, right_all), (warm, warm_all))
    pairs = []
    for g, (src, _) in enumerate(arrays):
        c = pltpu.make_async_remote_copy(src_ref=src.at[1 - core], dst_ref=paired.at[g], send_sem=pair_s.at[g],
                                         recv_sem=pair_r.at[g], device_id=partner, device_id_type=MESH)
        c.start()
        pairs.append(c)
    xcopies = []
    for src, dst, k in ((left, left_all, 0), (corner, corner_all, 1)):
        for d in (1, 2, 3):
            c = pltpu.make_async_remote_copy(
                src_ref=src, dst_ref=dst.at[x], send_sem=x_s.at[k, d - 1], recv_sem=x_r.at[k, d - 1],
                device_id=(wide_of(y, z, core), lax.rem(x + d, 4)), device_id_type=MESH)
            c.start()
            xcopies.append(c)
    own_x = []
    for src, dst, k in ((left, left_all, 0), (corner, corner_all, 1)):
        c = pltpu.make_async_copy(src, dst.at[x], own_s.at[2 + k])
        c.start()
        own_x.append(c)

    bounds = ((0, A_LANES), (A_LANES, HALF))

    def view(g, half, part, yy, zz):
        lo, hi = bounds[part]
        rows = pl.ds(pl.multiple_of((yy * 8 + zz) * SLOT, SLOT), SLOT)
        return arrays[g][1].at[half, rows, lo:hi]

    def slot(yy, zz):
        return yy * 8 + zz

    def send(g, part, yy, zz, sem, device, src=None):
        v = view(g, core, part, yy, zz)
        push(v if src is None else src, v, sem.at[g, part, slot(yy, zz)], ring_r.at[g, part, slot(yy, zz)], device)

    def forward_partner(g, part, yy, zz, src=None):
        v = view(g, core, part, yy, zz)
        push(v if src is None else src, v, part_s.at[g, part, slot(yy, zz)], part_r.at[g, part, slot(yy, zz)], partner)

    def arrived(g, part, yy, zz):
        v = view(g, core, part, yy, zz)
        pltpu.make_async_copy(v, v, ring_r.at[g, part, slot(yy, zz)]).wait()

    own_copies = []
    znext, zprev = at(y, zmove(1)), at(y, zmove(-1))
    ynext, yprev = at(ymove(1), z), at(ymove(-1), z)

    def begin(g):
        pairs[g].wait()
        merged[g] = paired[g] + arrays[g][0][core]
        c = pltpu.make_async_copy(
            merged.at[g], arrays[g][1].at[core, pl.ds(pl.multiple_of((y * 8 + z) * SLOT, SLOT), SLOT), :], own_s.at[g])
        c.start()
        own_copies.append(c)
        a, b = merged.at[g, :, 0:A_LANES], merged.at[g, :, A_LANES:HALF]
        va = view(g, core, 0, y, z)
        for d in (1, 2, 3):
            push(a, va, first_s.at[g, d - 1], ring_r.at[g, 0, slot(y, z)], at(ymove(d), z))
        send(g, 1, y, z, near_s, znext, b)
        send(g, 1, y, z, far_s, zprev, b)
        send(g, 0, y, z, near_s, znext, a)
        send(g, 0, y, z, far_s, zprev, a)
        send(g, 1, y, z, yl_s, ynext, b)
        send(g, 1, y, z, ys_s, yprev, b)
        forward_partner(g, 0, y, z, a)
        forward_partner(g, 1, y, z, b)

    def column(g):
        for d in (1, 2, 3):
            yy = ymove(d)
            arrived(g, 0, yy, z)
            send(g, 0, yy, z, near_s, znext)
            send(g, 0, yy, z, far_s, zprev)
            forward_partner(g, 0, yy, z)

    def b_ring(g, s, way):
        zz = zmove(-s) if way > 0 else zmove(s)
        arrived(g, 1, y, zz)
        if way > 0 and s < 4:
            send(g, 1, y, zz, near_s, znext)
        if way < 0 and s < 3:
            send(g, 1, y, zz, far_s, zprev)
        send(g, 1, y, zz, yl_s, ynext)
        send(g, 1, y, zz, ys_s, yprev)
        forward_partner(g, 1, y, zz)

    def a_ring(g, s, way, d):
        zz = zmove(-s) if way > 0 else zmove(s)
        yy = ymove(d)
        arrived(g, 0, yy, zz)
        if way > 0 and s < 4:
            send(g, 0, yy, zz, near_s, znext)
        if way < 0 and s < 3:
            send(g, 0, yy, zz, far_s, zprev)
        forward_partner(g, 0, yy, zz)

    def y_pass(g, zz):
        arrived(g, 1, ymove(-1), zz)
        send(g, 1, ymove(-1), zz, yl_s, ynext)
        forward_partner(g, 1, ymove(-1), zz)
        arrived(g, 1, ymove(1), zz)
        forward_partner(g, 1, ymove(1), zz)

    def y_last(g, zz):
        arrived(g, 1, ymove(2), zz)
        forward_partner(g, 1, ymove(2), zz)

    def ring_steps(g):
        steps = [lambda: y_pass(g, z)]
        for k in (1, 2, 3, 4):
            for way in (1, -1):
                if way < 0 and k == 4:
                    continue
                steps.append(functools.partial(b_ring, g, k, way))
                steps.extend(functools.partial(a_ring, g, k, way, d) for d in range(4))
            if k > 1:
                steps.append(functools.partial(y_pass, g, zmove(-(k - 1))))
                steps.append(functools.partial(y_pass, g, zmove(k - 1)))
        steps.append(lambda: y_pass(g, zmove(-4)))
        steps.extend(functools.partial(y_last, g, zmove(k)) for k in range(8))
        return steps

    def from_partner(g):
        for part in (0, 1):
            for k in range(32):
                v = view(g, 1 - core, part, k // 8, k % 8)
                pltpu.make_async_copy(v, v, part_r.at[g, part, k]).wait()

    begin(0)
    weights(layer, ket, bra)
    column(0)
    steps = ring_steps(0)
    for step in steps[:-17]:
        step()
    begin(1)
    for step in steps[-17:]:
        step()
    column(1)
    for c in xcopies + own_x:
        c.wait()
    acc = jnp.zeros((ROWS, 512), jnp.float32)
    for n in range(4):
        acc += jnp.dot(left_all[n], corner_all[n], preferred_element_type=jnp.float32)
    half[...] = acc.astype(jnp.bfloat16)
    own_copies[0].wait()
    from_partner(0)

    work = compute_steps(half, right_all, ket, bra, strip, layered)
    steps = ring_steps(1)
    done = 0
    for k, compute in enumerate(work):
        compute()
        upto = len(steps) * (k + 1) // len(work)
        for step in steps[done:upto]:
            step()
        done = upto
    own_copies[1].wait()
    from_partner(1)
    project(strip, warm_all, total, out)
    for c in pending:
        c.wait_send()


def iota(shape, axis):
    return lax.broadcasted_iota(jnp.int32, shape, axis)


def flags(mask):
    return jnp.where(mask, 1.0, 0.0).astype(jnp.bfloat16)


def mm(a, b):
    return jnp.dot(a, b, preferred_element_type=jnp.float32).astype(jnp.bfloat16)


def mm_nt(a, b):
    return lax.dot_general(a, b, (((1,), (1,)), ((), ())), preferred_element_type=jnp.float32).astype(jnp.bfloat16)


def weights(layer, ket, bra):
    row, col = iota((784, 49), 0), iota((784, 49), 1)
    low = row & 15
    spread = mm_nt(flags((row >> 4 == col) & (low < 7)), layer[0])
    spread += mm_nt(flags((row >> 4 == col) & (low >= 7) & (low < 14)), layer[1])
    row, col = iota((49, ROWS), 0), iota((49, ROWS), 1)
    q, u = col >> 3, col & 7
    full = mm(spread, flags((u < 7) & (q < 49) & (row == u * 7 + ((q * 37) >> 8))))
    row, col = iota((784, ROWS), 0), iota((784, ROWS), 1)
    low, q = row & 15, col >> 3
    same = jnp.where(low < 7, low, low - 7) == q - 7 * ((q * 37) >> 8)
    ket[...] = jnp.where(same, full.astype(jnp.float32), 0.0).astype(jnp.bfloat16)
    row, col = iota((56, 49), 0), iota((56, 49), 1)
    lead = flags((row & 7 < 7) & (col == (row & 7) * 7 + (row >> 3)))
    row, col = iota((49, 112), 0), iota((49, 112), 1)
    low = col & 15
    acc = jnp.zeros((56, 112), jnp.float32)
    for s in range(2):
        ok = (low >= 7 * s) & (low < 7 * s + 7) & (row == (col >> 4) * 7 + low - 7 * s)
        acc += mm(mm_nt(lead, layer[s]), flags(ok)).astype(jnp.float32)
    bra[...] = acc.astype(jnp.bfloat16)


def compute_steps(half, right, ket, bra, strip, layered):
    def strips(h, chunk):
        res = jnp.dot(half[...], right[h, :, chunk * 640:(chunk + 1) * 640], preferred_element_type=jnp.float32)
        for j in range(5):
            first = (h * 25 + chunk * 5 + j) * 8
            strip[:, first:first + 8, :] = res[:, j * 128:(j + 1) * 128].reshape(50, 8, 128)

    def kets(first):
        @pl.loop(first, first + 5)
        def _(t):
            x = jnp.concatenate([strip[2 * t].astype(jnp.bfloat16), strip[2 * t + 1].astype(jnp.bfloat16)], axis=1)
            res = jnp.dot(ket[...], x, preferred_element_type=jnp.float32).astype(jnp.bfloat16)
            for j in range(2):
                rows = pl.ds(pl.multiple_of((2 * t + j) * 16, 16), 16)
                layered[:, rows, :] = res[:, j * 128:(j + 1) * 128].reshape(49, 16, 128)

    def clear():
        strip[49] = jnp.zeros((ROWS, 128), jnp.float32)
        strip[:, 392:400, :] = jnp.zeros((50, 8, 128), jnp.float32)

    def bras(d):
        @pl.loop(0, 7)
        def _(r):
            x = jnp.concatenate([layered[d * 7 + r, i * 112:(i + 1) * 112, :] for i in range(7)], axis=1)
            res = jnp.dot(bra[...], x, preferred_element_type=jnp.float32)
            for i in range(7):
                for s in range(7):
                    strip[r * 7 + s, (i * 7 + d) * 8:(i * 7 + d) * 8 + 8, :] = (
                        res[s * 8:(s + 1) * 8, i * 128:(i + 1) * 128])

    work = [functools.partial(strips, h, chunk) for h in range(2) for chunk in range(5)]
    work += [functools.partial(kets, 5 * t) for t in range(5)]
    work += [clear]
    work += [functools.partial(bras, d) for d in range(7)]
    return work


def project(enlarged, warm, total, out):
    total[...] = jnp.zeros_like(total)
    for h in range(2):
        @pl.loop(0, 5)
        def _(chunk):
            cols = pl.ds(pl.multiple_of(chunk * 640, 640), 640)
            x = jnp.concatenate(
                [enlarged[h * 25 + chunk * 5 + j].astype(jnp.bfloat16) for j in range(5)], axis=1)
            total[...] += lax.dot_general(x, warm[h, :, cols], (((1,), (1,)), ((), ())),
                                          preferred_element_type=jnp.float32)
    row, col = iota((512, 512), 0), iota((512, 512), 1)
    held = jnp.where(row & 15 < 14, (row >> 4) * 14 + (row & 15), -1)
    pick = flags(held == jnp.where(col & 127 < 112, (col >> 7) * 112 + (col & 127), -2))
    res = mm(total[...].astype(jnp.bfloat16), pick)
    for n in range(4):
        out[n] = res[:, n * 128:(n + 1) * 128]


def gathers(right, warm, left, corner, layer):
    dma = pltpu.SemaphoreType.DMA
    vm = pl.BlockSpec(memory_space=pltpu.VMEM)
    return pl.pallas_call(
        gather_kernel,
        out_shape=jax.ShapeDtypeStruct((4, ROWS, 128), jnp.bfloat16),
        in_specs=[vm] * 5,
        out_specs=vm,
        scratch_shapes=[
            pltpu.VMEM((2, 32 * SLOT, HALF), jnp.bfloat16),
            pltpu.VMEM((2, 32 * SLOT, HALF), jnp.bfloat16),
            pltpu.VMEM((4, ROWS, 128), jnp.bfloat16),
            pltpu.VMEM((4, 128, 512), jnp.bfloat16),
            pltpu.VMEM((ROWS, 512), jnp.bfloat16),
            pltpu.VMEM((50, ROWS, 128), jnp.float32),
            pltpu.VMEM((49, 800, 128), jnp.bfloat16),
            pltpu.VMEM((ROWS, 512), jnp.float32),
            pltpu.VMEM((784, ROWS), jnp.bfloat16),
            pltpu.VMEM((56, 112), jnp.bfloat16),
            pltpu.VMEM((2, SLOT, HALF), jnp.bfloat16),
            pltpu.VMEM((2, SLOT, HALF), jnp.bfloat16),
            dma((2,)), dma((2,)), dma((4,)), dma((2, 2, 32)), dma((2, 2, 32)), dma((2, 2, 32)),
            dma((2, 2, 32)), dma((2, 2, 32)), dma((2, 3)), dma((2, 2, 32)), dma((2, 2, 32)), dma((2, 3)), dma((2, 3)),
        ],
        compiler_params=pltpu.CompilerParams(collective_id=1, has_side_effects=True, vmem_limit_bytes=58 * MIB),
        name="gathers",
    )(right, warm, left, corner, layer)


def sums_kernel(part, proj, gram, got, slab, got1, piece, got2, n_s, n_r, p_s, p_r, a_s, a_r, b_s, b_r,
                c_s, c_r, d_s, d_r, e_s, e_r, f_s, f_r):
    y, z, core, x = place()
    others = [(lax.rem(y + k // 2, 4), lax.rem(core + k % 2, 2)) for k in range(1, 8)]
    xs = [lax.rem(x + d, 4) for d in (1, 2, 3)]
    zs = [lax.rem(z + d, 8) for d in range(1, 8)]
    me = wide_of(y, z, core)
    greet([(me, xx) for xx in xs] + [(wide_of(yy, z, cc), x) for yy, cc in others]
          + [(wide_of(y, zz, core), x) for zz in zs])

    def start(src, dst, ss, rs, device):
        c = pltpu.make_async_remote_copy(src_ref=src, dst_ref=dst, send_sem=ss, recv_sem=rs,
                                         device_id=device, device_id_type=MESH)
        c.start()
        return c

    c1 = [start(part.at[xs[d]], got.at[d], n_s.at[d], n_r.at[d], (me, xs[d])) for d in range(3)]
    acc = part[x].astype(jnp.float32)
    for d in range(3):
        c1[d].wait_recv()
        acc += got[d].astype(jnp.float32)
    proj[x] = acc.astype(jnp.bfloat16)
    c2 = [start(proj.at[x], proj.at[x], p_s.at[d], p_r.at[d], (me, xs[d])) for d in range(3)]
    own = acc.astype(jnp.bfloat16)
    tn = (((0,), (0,)), ((), ()))
    scale = 1.0 / (448 * 49)

    def product(n):
        slab[pl.ds(pl.multiple_of(n * 128, 128), 128), :] = lax.dot_general(
            proj[n], own, tn, preferred_element_type=jnp.float32) * scale

    product(x)
    for d in (0, 2, 1):
        c2[d].wait_recv()
        product(lax.rem(x + 3 - d, 4))

    def rows(k, size):
        return pl.ds(pl.multiple_of(k * size, size), size)

    mine = y * 2 + core
    c3 = [start(slab.at[rows(yy * 2 + cc, 64)], got1.at[k], a_s.at[k], a_r.at[k], (wide_of(yy, z, cc), x))
          for k, (yy, cc) in enumerate(others)]
    acc = slab[rows(mine, 64), :]
    for k in range(7):
        c3[k].wait_recv()
        acc += got1[k]
    piece[...] = acc
    c4 = [start(piece.at[rows(zz, 8)], got2.at[k], b_s.at[k], b_r.at[k], (wide_of(y, zz, core), x))
          for k, zz in enumerate(zs)]
    acc = piece[rows(z, 8), :]
    for k in range(7):
        c4[k].wait_recv()
        acc += got2[k]
    spot = gram.at[x, y, core, rows(z, 8)]
    gram[x, y, core, rows(z, 8), :] = acc
    c5 = [start(spot, spot, c_s.at[k], c_r.at[k], (wide_of(y, zz, core), x)) for k, zz in enumerate(zs)]
    for c in c5:
        c.wait_recv()
    spot = gram.at[x, y, core]
    c6 = [start(spot, spot, d_s.at[d], d_r.at[d], (me, xs[d])) for d in range(3)]
    for c in c6:
        c.wait_recv()
    spot = gram.at[:, y, core]
    c7 = [start(spot, spot, e_s.at[d - 1], e_r.at[d - 1], (wide_of(lax.rem(y + d, 4), z, core), x)) for d in (1, 2, 3)]
    other = (wide_of(y, z, 1 - core), x)
    c8 = [start(spot, spot, f_s.at[0], f_r.at[0], other)]
    for d in (3, 1, 2):
        c7[d - 1].wait_recv()
        spot = gram.at[:, lax.rem(y + 4 - d, 4), core]
        c8.append(start(spot, spot, f_s.at[d], f_r.at[d], other))
    for c in c8:
        c.wait()
    for c in c1 + c2 + c3 + c4 + c5 + c6 + c7:
        c.wait_send()


def sums(part):
    dma = pltpu.SemaphoreType.DMA
    vm = pl.BlockSpec(memory_space=pltpu.VMEM)
    return pl.pallas_call(
        sums_kernel,
        out_shape=[
            jax.ShapeDtypeStruct((4, ROWS, 128), jnp.bfloat16),
            jax.ShapeDtypeStruct((4, 4, 2, 64, 128), jnp.float32),
        ],
        in_specs=[vm],
        out_specs=[vm, vm],
        scratch_shapes=[
            pltpu.VMEM((3, ROWS, 128), jnp.bfloat16),
            pltpu.VMEM((512, 128), jnp.float32),
            pltpu.VMEM((7, 64, 128), jnp.float32),
            pltpu.VMEM((64, 128), jnp.float32),
            pltpu.VMEM((7, 8, 128), jnp.float32),
            dma((3,)), dma((3,)), dma((3,)), dma((3,)), dma((7,)), dma((7,)), dma((7,)), dma((7,)),
            dma((7,)), dma((7,)), dma((3,)), dma((3,)), dma((3,)), dma((3,)), dma((4,)), dma((4,)),
        ],
        compiler_params=pltpu.CompilerParams(collective_id=2, has_side_effects=True, vmem_limit_bytes=32 * MIB),
        name="sums",
    )(part)


def eliminate(diag):
    n = BLOCK
    row_id = lax.broadcasted_iota(jnp.int32, (n, n), 0)
    col_id = lax.broadcasted_iota(jnp.int32, (n, n), 1)
    eye = jnp.where(row_id == col_id, 1.0, 0.0).astype(jnp.float32)
    wide = jnp.concatenate([diag, eye], axis=1)
    groups = [wide[8 * g:8 * g + 8] for g in range(n // 8)]
    sub = lax.broadcasted_iota(jnp.int32, (8, 2 * n), 0)
    for k in range(n):
        g, t = divmod(k, 8)
        pivot = groups[g][t:t + 1, :]
        scaled = pivot * (1.0 / pivot[:, k:k + 1])
        for h in range(g, n // 8):
            if h == g and t == 7:
                continue
            update = groups[h][:, k:k + 1] * scaled
            if h == g:
                update = jnp.where(sub > t, update, 0.0)
            groups[h] = groups[h] - update
    wide = jnp.concatenate(groups, axis=0)
    upper, lower = wide[:, :n], wide[:, n:]
    d = jnp.sum(upper * eye, axis=1, keepdims=True)
    root = lax.rsqrt(d)
    root = root * (1.5 - 0.5 * d * root * root)
    return jnp.where(row_id <= col_id, upper * root, 0.0), jnp.where(row_id >= col_id, lower * root, 0.0)


def factor_kernel(gram, proj, r_ref, out, work):
    n = 448
    x = lax.axis_index("narrow")
    for a in range(4):
        for b in range(4):
            work[a * 112:(a + 1) * 112, b * 112:(b + 1) * 112] = gram[b, a * 128:a * 128 + 112, 0:112]
    r_ref[...] = jnp.zeros_like(r_ref)
    col = lax.broadcasted_iota(jnp.int32, (BLOCK, n), 1)
    row = lax.broadcasted_iota(jnp.int32, (BLOCK, n), 0)
    for b in range(n // BLOCK):
        lo, hi = b * BLOCK, (b + 1) * BLOCK
        r, inverse = eliminate(work[lo:hi, lo:hi])
        inside = (col >= lo) & (col < hi)
        src = jnp.where(inside, jnp.where(col - lo == row, 1.0, 0.0), work[lo:hi, :])
        full = jnp.dot(inverse, src, precision=HI, preferred_element_type=jnp.float32)
        work[lo:hi, :] = jnp.where(col < hi, full, 0.0)
        rest = jnp.where(col >= hi, full, 0.0)
        r_ref[lo:hi, :] = rest
        r_ref[lo:hi, lo:hi] = r
        if hi < n:
            at = lax.broadcasted_iota(jnp.int32, (n - hi, n), 1)
            old = jnp.where((at >= lo) & (at < hi), 0.0, work[hi:, :])
            work[hi:, :] = old - lax.dot_general(rest[:, hi:], full, (((0,), (0,)), ((), ())), precision=HI,
                                                 preferred_element_type=jnp.float32)
    own = work[pl.ds(pl.multiple_of(x * 112, 8), 112), :]
    nt = (((1,), (1,)), ((), ()))
    acc = jnp.zeros((ROWS, 112), jnp.float32)
    for b in range(4):
        acc += lax.dot_general(proj[b][:, 0:112].astype(jnp.float32), own[:, b * 112:(b + 1) * 112], nt, precision=HI,
                               preferred_element_type=jnp.float32)
    out[...] = acc


def factor(gram, proj):
    vm = pl.BlockSpec(memory_space=pltpu.VMEM)
    return pl.pallas_call(
        factor_kernel,
        out_shape=[jax.ShapeDtypeStruct((448, 448), jnp.float32), jax.ShapeDtypeStruct((ROWS, 112), jnp.float32)],
        in_specs=[vm, vm],
        out_specs=[vm, vm],
        scratch_shapes=[pltpu.VMEM((448, 448), jnp.float32)],
        compiler_params=pltpu.CompilerParams(vmem_limit_bytes=40 * MIB),
        name="factor",
    )(gram, proj)


def shard_rows(block, core):
    rows = jnp.pad(block, ((0, 0), (0, 1), (0, 16))).reshape(7, 2, HALF).transpose(1, 0, 2)
    return jnp.where(core == 0, jnp.pad(rows, ((0, 0), (0, 9), (0, 0))), jnp.pad(rows, ((0, 0), (7, 2), (0, 0))))


def on_device(left_edge, corner, right_edge, single_layer, warm_basis):
    core = lax.axis_index("wide") % 2
    right = shard_rows(right_edge, core)
    warm = shard_rows(warm_basis.transpose(2, 0, 1), core)
    left = left_edge.reshape(7, 7, 7, 112).transpose(0, 2, 1, 3)
    left = jnp.pad(left, ((0, 0), (0, 0), (0, 1), (0, 16))).reshape(392, 128)
    left = jnp.pad(left, ((0, 8), (0, 0)))
    corner = jnp.pad(corner.reshape(112, 32, 14), ((0, 16), (0, 0), (0, 2))).reshape(128, 512)
    part = gathers(right, warm, left, corner, single_layer.reshape(2, 49, 49))
    proj, gram = sums(part)
    r_factor, rows = factor(gram.reshape(4, 512, 128), proj)
    new_basis = rows[:392].reshape(7, 7, 8, 112)[:, :, :7].reshape(7, 49, 112)
    return new_basis, r_factor


def solution(mesh):
    placed = (
        P("wide", None, "narrow"),
        P("narrow", None),
        P("wide", None, "narrow"),
        P(),
        P(None, "narrow", "wide"),
    )
    return jax.shard_map(
        on_device,
        mesh=mesh,
        in_specs=placed,
        out_specs=(P("wide", None, "narrow"), P()),
        check_vma=False,
    )
```

```python
import functools

import jax
import jax.numpy as jnp
from jax import lax
from jax.experimental import pallas as pl
from jax.experimental.pallas import tpu as pltpu
from jax.sharding import PartitionSpec as P

BOND = 7
BLOCK = 64
SLOT = 16
HALF = 3200
A_LANES = 1280
ROWS = 400
HI = lax.Precision.HIGHEST
MESH = pl.DeviceIdType.MESH
MIB = 1 << 20


def place():
    wide = lax.axis_index("wide")
    core = lax.rem(wide, 2)
    z = lax.rem(lax.div(wide, 2), 8)
    y = lax.div(wide, 16)
    return y, z, core, lax.axis_index("narrow")


def wide_of(y, z, core):
    return (y * 8 + z) * 2 + core


def greet(peers):
    barrier = pltpu.get_barrier_semaphore()
    for peer in peers:
        pl.semaphore_signal(barrier, inc=1, device_id=peer, device_id_type=MESH)
    pl.semaphore_wait(barrier, len(peers))


def gather_kernel(right, warm, left, corner, layer, proj, gram,
                  right_all, warm_all, left_all, corner_all, half, strip, layered, total, ket, bra,
                  paired, merged, part, got, slab, got1, piece, got2,
                  pair_s, pair_r, own_s, ring_r, ring_s, part_s, part_r, x_s, x_r,
                  n_s, n_r, p_s, p_r, a_s, a_r, b_s, b_r, c_s, c_r, d_s, d_r, f_s, f_r):
    y, z, core, x = place()
    zdir = 1 - 2 * core

    def zmove(k):
        return lax.rem(z + 8 + k * zdir, 8)

    def ymove(k):
        return lax.rem(y + 4 + k * zdir, 4)

    def at(yy, zz, cc=None):
        return (wide_of(yy, zz, core if cc is None else cc), x)

    partner = at(y, z, 1 - core)
    others = [(lax.rem(y + k // 2, 4), lax.rem(core + k % 2, 2)) for k in range(1, 8)]
    xs = [lax.rem(x + d, 4) for d in (1, 2, 3)]
    zs = [lax.rem(z + d, 8) for d in range(1, 8)]
    me = wide_of(y, z, core)
    plane = [(lax.rem(x + k // 4, 4), lax.rem(y + k % 4, 4)) for k in (10, 2, 8, 6, 14, 9, 11, 1, 3, 4, 12, 5, 7, 13, 15)]
    greet([at(yy, z, cc) for yy, cc in others] + [at(y, zz) for zz in zs]
          + [(wide_of(lax.rem(y + k % 4, 4), z, core), lax.rem(x + k // 4, 4)) for k in range(4, 16)])

    def push(src, dst, ss, rs, device):
        c = pltpu.make_async_remote_copy(src_ref=src, dst_ref=dst, send_sem=ss, recv_sem=rs,
                                         device_id=device, device_id_type=MESH)
        c.start()

    arrays = ((right, right_all), (warm, warm_all))
    pairs = []
    for g, (src, _) in enumerate(arrays):
        c = pltpu.make_async_remote_copy(src_ref=src.at[1 - core], dst_ref=paired.at[g], send_sem=pair_s.at[g],
                                         recv_sem=pair_r.at[g], device_id=partner, device_id_type=MESH)
        c.start()
        pairs.append(c)
    xcopies = []
    for src, dst, k in ((left, left_all, 0), (corner, corner_all, 1)):
        for d in (1, 2, 3):
            c = pltpu.make_async_remote_copy(
                src_ref=src, dst_ref=dst.at[x], send_sem=x_s.at[k, d - 1], recv_sem=x_r.at[k, d - 1],
                device_id=(wide_of(y, z, core), lax.rem(x + d, 4)), device_id_type=MESH)
            c.start()
            xcopies.append(c)
    own_x = []
    for src, dst, k in ((left, left_all, 0), (corner, corner_all, 1)):
        c = pltpu.make_async_copy(src, dst.at[x], own_s.at[2 + k])
        c.start()
        own_x.append(c)

    bounds = ((0, A_LANES), (A_LANES, HALF))

    def view(g, half, part, yy, zz):
        lo, hi = bounds[part]
        rows = pl.ds(pl.multiple_of((yy * 8 + zz) * SLOT, SLOT), SLOT)
        return arrays[g][1].at[half, rows, lo:hi]

    def slot(yy, zz):
        return yy * 8 + zz

    def send(g, part, yy, zz, device, src=None):
        v = view(g, core, part, yy, zz)
        push(v if src is None else src, v, ring_s.at[g], ring_r.at[g, part, slot(yy, zz)], device)

    def forward_partner(g, part, yy, zz, src=None):
        v = view(g, core, part, yy, zz)
        push(v if src is None else src, v, part_s.at[g], part_r.at[g], partner)

    def arrived(g, part, yy, zz):
        v = view(g, core, part, yy, zz)
        pltpu.make_async_copy(v, v, ring_r.at[g, part, slot(yy, zz)]).wait()

    own_copies = []
    znext, zprev = at(y, zmove(1)), at(y, zmove(-1))
    ynext, yprev = at(ymove(1), z), at(ymove(-1), z)

    def begin(g):
        pairs[g].wait()
        merged[g] = paired[g] + arrays[g][0][core]
        c = pltpu.make_async_copy(
            merged.at[g], arrays[g][1].at[core, pl.ds(pl.multiple_of((y * 8 + z) * SLOT, SLOT), SLOT), :], own_s.at[g])
        c.start()
        own_copies.append(c)
        a, b = merged.at[g, :, 0:A_LANES], merged.at[g, :, A_LANES:HALF]
        va = view(g, core, 0, y, z)
        for d in (1, 2, 3):
            push(a, va, ring_s.at[g], ring_r.at[g, 0, slot(y, z)], at(ymove(d), z))
        send(g, 1, y, z, znext, b)
        send(g, 1, y, z, zprev, b)
        send(g, 0, y, z, znext, a)
        send(g, 0, y, z, zprev, a)
        send(g, 1, y, z, ynext, b)
        send(g, 1, y, z, yprev, b)
        forward_partner(g, 0, y, z, a)
        forward_partner(g, 1, y, z, b)

    def column(g):
        for d in (1, 2, 3):
            yy = ymove(d)
            arrived(g, 0, yy, z)
            send(g, 0, yy, z, znext)
            send(g, 0, yy, z, zprev)
            forward_partner(g, 0, yy, z)

    def b_ring(g, s, way):
        zz = zmove(-s) if way > 0 else zmove(s)
        arrived(g, 1, y, zz)
        if way > 0 and s < 4:
            send(g, 1, y, zz, znext)
        if way < 0 and s < 3:
            send(g, 1, y, zz, zprev)
        send(g, 1, y, zz, ynext)
        send(g, 1, y, zz, yprev)
        forward_partner(g, 1, y, zz)

    def a_ring(g, s, way, d):
        zz = zmove(-s) if way > 0 else zmove(s)
        yy = ymove(d)
        arrived(g, 0, yy, zz)
        if way > 0 and s < 4:
            send(g, 0, yy, zz, znext)
        if way < 0 and s < 3:
            send(g, 0, yy, zz, zprev)
        forward_partner(g, 0, yy, zz)

    def y_pass(g, zz):
        arrived(g, 1, ymove(-1), zz)
        send(g, 1, ymove(-1), zz, ynext)
        forward_partner(g, 1, ymove(-1), zz)
        arrived(g, 1, ymove(1), zz)
        forward_partner(g, 1, ymove(1), zz)

    def y_last(g, zz):
        arrived(g, 1, ymove(2), zz)
        forward_partner(g, 1, ymove(2), zz)

    def ring_steps(g):
        steps = [lambda: y_pass(g, z)]
        for k in (1, 2, 3, 4):
            for way in (1, -1):
                if way < 0 and k == 4:
                    continue
                steps.append(functools.partial(b_ring, g, k, way))
                steps.extend(functools.partial(a_ring, g, k, way, d) for d in range(4))
            if k > 1:
                steps.append(functools.partial(y_pass, g, zmove(-(k - 1))))
                steps.append(functools.partial(y_pass, g, zmove(k - 1)))
        steps.append(lambda: y_pass(g, zmove(-4)))
        steps.extend(functools.partial(y_last, g, zmove(k)) for k in range(8))
        return steps

    def from_partner(g):
        settle(arrays[g][1].at[1 - core], part_r.at[g])

    def settle(ref, sem):
        pltpu.make_async_copy(ref, ref, sem).wait()

    begin(0)
    weights(layer, ket, bra)
    column(0)
    steps = ring_steps(0)
    for step in steps[:-17]:
        step()
    begin(1)
    for step in steps[-17:]:
        step()
    column(1)
    for c in xcopies + own_x:
        c.wait()
    acc = jnp.zeros((ROWS, 512), jnp.float32)
    for n in range(4):
        acc += jnp.dot(left_all[n], corner_all[n], preferred_element_type=jnp.float32)
    half[...] = acc.astype(jnp.bfloat16)
    own_copies[0].wait()
    from_partner(0)

    work = compute_steps(half, right_all, ket, bra, strip, layered)
    steps = ring_steps(1)
    done = 0
    for k, compute in enumerate(work):
        compute()
        upto = len(steps) * (k + 1) // len(work)
        for step in steps[done:upto]:
            step()
        done = upto
    own_copies[1].wait()
    from_partner(1)

    def start(src, dst, ss, rs, device):
        c = pltpu.make_async_remote_copy(src_ref=src, dst_ref=dst, send_sem=ss, recv_sem=rs,
                                         device_id=device, device_id_type=MESH)
        c.start()
        return c

    c1 = [None] * 3
    for pair in ((1, 0), (2, None)):
        names = [x if d is None else xs[d] for d in pair]
        project(strip, warm_all, total, part, names)
        for d in pair:
            if d is not None:
                c1[d] = start(part.at[xs[d]], got.at[d], n_s.at[d], n_r.at[d], (me, xs[d]))
    acc = part[x].astype(jnp.float32)
    for d in range(3):
        c1[d].wait_recv()
        acc += got[d].astype(jnp.float32)
    proj[x] = acc.astype(jnp.bfloat16)
    c2 = [start(proj.at[x], proj.at[x], p_s.at[d], p_r.at[d], (me, xs[d])) for d in range(3)]
    own = acc.astype(jnp.bfloat16)
    tn = (((0,), (0,)), ((), ()))
    scale = 1.0 / (448 * 49)

    def product(n):
        slab[pl.ds(pl.multiple_of(n * 128, 128), 128), :] = lax.dot_general(
            proj[n], own, tn, preferred_element_type=jnp.float32) * scale

    product(x)
    for d in (0, 2, 1):
        c2[d].wait_recv()
        product(lax.rem(x + 3 - d, 4))

    def rows(k, size):
        return pl.ds(pl.multiple_of(k * size, size), size)

    mine = y * 2 + core
    c3 = [start(slab.at[rows(yy * 2 + cc, 64)], got1.at[k], a_s.at[k], a_r.at[k], (wide_of(yy, z, cc), x))
          for k, (yy, cc) in enumerate(others)]
    acc = slab[rows(mine, 64), :]
    for k in range(7):
        c3[k].wait_recv()
        acc += got1[k]
    piece[...] = acc
    c4 = [start(piece.at[rows(zz, 8)], got2.at[k], b_s.at[k], b_r.at[k], (wide_of(y, zz, core), x))
          for k, zz in enumerate(zs)]
    acc = piece[rows(z, 8), :]
    for k in range(7):
        c4[k].wait_recv()
        acc += got2[k]
    spot = gram.at[x, y, core, rows(z, 8)]
    gram[x, y, core, rows(z, 8), :] = acc
    c5 = [start(spot, spot, c_s.at[k], c_r.at[k], at(y, zz)) for k, zz in enumerate(zs)]
    for c in c5:
        c.wait_recv()
    spot = gram.at[x, y, core]
    c6 = [start(spot, spot, d_s.at[k], d_r.at[k], (wide_of(yy, z, core), xx)) for k, (xx, yy) in enumerate(plane)]
    start(spot, spot, f_s, f_r, partner)
    for k in (7, 8, 9, 10, 2, 1, 11, 12, 13, 14, 3, 4, 5, 6, 0):
        xx, yy = plane[k]
        c6[k].wait_recv()
        spot = gram.at[lax.rem(2 * x + 4 - xx, 4), lax.rem(2 * y + 4 - yy, 4), core]
        start(spot, spot, f_s, f_r, partner)
    settle(gram.at[:, :, core], f_s)
    settle(gram.at[:, :, 1 - core], f_r)
    for c in c1 + c2 + c3 + c4 + c5 + c6:
        c.wait_send()
    for g in (0, 1):
        settle(arrays[g][1].at[core], part_s.at[g])
        settle(arrays[g][1].at[core, 0:496], ring_s.at[g])


def iota(shape, axis):
    return lax.broadcasted_iota(jnp.int32, shape, axis)


def flags(mask):
    return jnp.where(mask, 1.0, 0.0).astype(jnp.bfloat16)


def mm(a, b):
    return jnp.dot(a, b, preferred_element_type=jnp.float32).astype(jnp.bfloat16)


def mm_nt(a, b):
    return lax.dot_general(a, b, (((1,), (1,)), ((), ())), preferred_element_type=jnp.float32).astype(jnp.bfloat16)


def weights(layer, ket, bra):
    row, col = iota((784, 49), 0), iota((784, 49), 1)
    low = row & 15
    spread = mm_nt(flags((row >> 4 == col) & (low < 7)), layer[0])
    spread += mm_nt(flags((row >> 4 == col) & (low >= 7) & (low < 14)), layer[1])
    row, col = iota((49, ROWS), 0), iota((49, ROWS), 1)
    q, u = col >> 3, col & 7
    full = mm(spread, flags((u < 7) & (q < 49) & (row == u * 7 + ((q * 37) >> 8))))
    row, col = iota((784, ROWS), 0), iota((784, ROWS), 1)
    low, q = row & 15, col >> 3
    same = jnp.where(low < 7, low, low - 7) == q - 7 * ((q * 37) >> 8)
    ket[...] = jnp.where(same, full.astype(jnp.float32), 0.0).astype(jnp.bfloat16)
    row, col = iota((56, 49), 0), iota((56, 49), 1)
    lead = flags((row & 7 < 7) & (col == (row & 7) * 7 + (row >> 3)))
    row, col = iota((49, 112), 0), iota((49, 112), 1)
    low = col & 15
    acc = jnp.zeros((56, 112), jnp.float32)
    for s in range(2):
        ok = (low >= 7 * s) & (low < 7 * s + 7) & (row == (col >> 4) * 7 + low - 7 * s)
        acc += mm(mm_nt(lead, layer[s]), flags(ok)).astype(jnp.float32)
    bra[...] = acc.astype(jnp.bfloat16)


def compute_steps(half, right, ket, bra, strip, layered):
    def strips(h, chunk):
        res = jnp.dot(half[...], right[h, :, chunk * 640:(chunk + 1) * 640], preferred_element_type=jnp.float32)
        for j in range(5):
            first = (h * 25 + chunk * 5 + j) * 8
            strip[:, first:first + 8, :] = res[:, j * 128:(j + 1) * 128].reshape(50, 8, 128)

    def kets(first):
        @pl.loop(first, first + 5)
        def _(t):
            x = jnp.concatenate([strip[2 * t].astype(jnp.bfloat16), strip[2 * t + 1].astype(jnp.bfloat16)], axis=1)
            res = jnp.dot(ket[...], x, preferred_element_type=jnp.float32).astype(jnp.bfloat16)
            for j in range(2):
                rows = pl.ds(pl.multiple_of((2 * t + j) * 16, 16), 16)
                layered[:, rows, :] = res[:, j * 128:(j + 1) * 128].reshape(49, 16, 128)

    def clear():
        strip[49] = jnp.zeros((ROWS, 128), jnp.float32)
        strip[:, 392:400, :] = jnp.zeros((50, 8, 128), jnp.float32)

    def bras(d):
        @pl.loop(0, 7)
        def _(r):
            x = jnp.concatenate([layered[d * 7 + r, i * 112:(i + 1) * 112, :] for i in range(7)], axis=1)
            res = jnp.dot(bra[...], x, preferred_element_type=jnp.float32)
            for i in range(7):
                for s in range(7):
                    strip[r * 7 + s, (i * 7 + d) * 8:(i * 7 + d) * 8 + 8, :] = (
                        res[s * 8:(s + 1) * 8, i * 128:(i + 1) * 128])

    work = [functools.partial(strips, h, chunk) for h in range(2) for chunk in range(5)]
    work += [functools.partial(kets, 5 * t) for t in range(5)]
    work += [clear]
    work += [functools.partial(bras, d) for d in range(7)]
    return work


def project(enlarged, warm, total, part, names):
    total[...] = jnp.zeros_like(total)
    spans = [pl.ds(pl.multiple_of(n * 128, 128), 128) for n in names]
    for h in range(2):
        @pl.loop(0, 5)
        def _(chunk):
            cols = pl.ds(pl.multiple_of(chunk * 640, 640), 640)
            x = jnp.concatenate(
                [enlarged[h * 25 + chunk * 5 + j].astype(jnp.bfloat16) for j in range(5)], axis=1)
            w = jnp.concatenate([warm[h, span, cols] for span in spans], axis=0)
            total[...] += lax.dot_general(x, w, (((1,), (1,)), ((), ())), preferred_element_type=jnp.float32)
    row, col = iota((128, 128), 0), iota((128, 128), 1)
    pick = flags((row & 15 < 14) & (col == (row >> 4) * 14 + (row & 15)))
    for k, n in enumerate(names):
        part[n] = mm(total[:, k * 128:(k + 1) * 128].astype(jnp.bfloat16), pick)


def gathers(right, warm, left, corner, layer):
    dma = pltpu.SemaphoreType.DMA
    vm = pl.BlockSpec(memory_space=pltpu.VMEM)
    return pl.pallas_call(
        gather_kernel,
        out_shape=[
            jax.ShapeDtypeStruct((4, ROWS, 128), jnp.bfloat16),
            jax.ShapeDtypeStruct((4, 4, 2, 64, 128), jnp.float32),
        ],
        in_specs=[vm] * 5,
        out_specs=[vm, vm],
        scratch_shapes=[
            pltpu.VMEM((2, 32 * SLOT, HALF), jnp.bfloat16),
            pltpu.VMEM((2, 32 * SLOT, HALF), jnp.bfloat16),
            pltpu.VMEM((4, ROWS, 128), jnp.bfloat16),
            pltpu.VMEM((4, 128, 512), jnp.bfloat16),
            pltpu.VMEM((ROWS, 512), jnp.bfloat16),
            pltpu.VMEM((50, ROWS, 128), jnp.float32),
            pltpu.VMEM((49, 800, 128), jnp.bfloat16),
            pltpu.VMEM((ROWS, 256), jnp.float32),
            pltpu.VMEM((784, ROWS), jnp.bfloat16),
            pltpu.VMEM((56, 112), jnp.bfloat16),
            pltpu.VMEM((2, SLOT, HALF), jnp.bfloat16),
            pltpu.VMEM((2, SLOT, HALF), jnp.bfloat16),
            pltpu.VMEM((4, ROWS, 128), jnp.bfloat16),
            pltpu.VMEM((3, ROWS, 128), jnp.bfloat16),
            pltpu.VMEM((512, 128), jnp.float32),
            pltpu.VMEM((7, 64, 128), jnp.float32),
            pltpu.VMEM((64, 128), jnp.float32),
            pltpu.VMEM((7, 8, 128), jnp.float32),
            dma((2,)), dma((2,)), dma((4,)), dma((2, 2, 32)), dma((2,)), dma((2,)), dma((2,)), dma((2, 3)), dma((2, 3)),
            dma((3,)), dma((3,)), dma((3,)), dma((3,)), dma((7,)), dma((7,)), dma((7,)), dma((7,)),
            dma((7,)), dma((7,)), dma((15,)), dma((15,)), dma, dma,
        ],
        compiler_params=pltpu.CompilerParams(collective_id=1, has_side_effects=True, vmem_limit_bytes=60 * MIB),
        name="gathers",
    )(right, warm, left, corner, layer)


def eliminate(diag):
    n = BLOCK
    row_id = lax.broadcasted_iota(jnp.int32, (n, n), 0)
    col_id = lax.broadcasted_iota(jnp.int32, (n, n), 1)
    eye = jnp.where(row_id == col_id, 1.0, 0.0).astype(jnp.float32)
    wide = jnp.concatenate([diag, eye], axis=1)
    groups = [wide[8 * g:8 * g + 8] for g in range(n // 8)]
    sub = lax.broadcasted_iota(jnp.int32, (8, 2 * n), 0)
    for k in range(n):
        g, t = divmod(k, 8)
        pivot = groups[g][t:t + 1, :]
        scaled = pivot * (1.0 / pivot[:, k:k + 1])
        for h in range(g, n // 8):
            if h == g and t == 7:
                continue
            update = groups[h][:, k:k + 1] * scaled
            if h == g:
                update = jnp.where(sub > t, update, 0.0)
            groups[h] = groups[h] - update
    wide = jnp.concatenate(groups, axis=0)
    upper, lower = wide[:, :n], wide[:, n:]
    d = jnp.sum(upper * eye, axis=1, keepdims=True)
    root = lax.rsqrt(d)
    root = root * (1.5 - 0.5 * d * root * root)
    return jnp.where(row_id <= col_id, upper * root, 0.0), jnp.where(row_id >= col_id, lower * root, 0.0)


def factor_kernel(gram, proj, r_ref, out, work):
    n = 448
    x = lax.axis_index("narrow")
    for a in range(4):
        for b in range(4):
            work[a * 112:(a + 1) * 112, b * 112:(b + 1) * 112] = gram[b, a * 128:a * 128 + 112, 0:112]
    r_ref[...] = jnp.zeros_like(r_ref)
    col = lax.broadcasted_iota(jnp.int32, (BLOCK, n), 1)
    row = lax.broadcasted_iota(jnp.int32, (BLOCK, n), 0)
    for b in range(n // BLOCK):
        lo, hi = b * BLOCK, (b + 1) * BLOCK
        r, inverse = eliminate(work[lo:hi, lo:hi])
        inside = (col >= lo) & (col < hi)
        src = jnp.where(inside, jnp.where(col - lo == row, 1.0, 0.0), work[lo:hi, :])
        full = jnp.dot(inverse, src, precision=HI, preferred_element_type=jnp.float32)
        work[lo:hi, :] = jnp.where(col < hi, full, 0.0)
        rest = jnp.where(col >= hi, full, 0.0)
        r_ref[lo:hi, :] = rest
        r_ref[lo:hi, lo:hi] = r
        if hi < n:
            at = lax.broadcasted_iota(jnp.int32, (n - hi, n), 1)
            old = jnp.where((at >= lo) & (at < hi), 0.0, work[hi:, :])
            work[hi:, :] = old - lax.dot_general(rest[:, hi:], full, (((0,), (0,)), ((), ())), precision=HI,
                                                 preferred_element_type=jnp.float32)
    own = work[pl.ds(pl.multiple_of(x * 112, 8), 112), :]
    nt = (((1,), (1,)), ((), ()))
    acc = jnp.zeros((ROWS, 112), jnp.float32)
    for b in range(4):
        acc += lax.dot_general(proj[b][:, 0:112].astype(jnp.float32), own[:, b * 112:(b + 1) * 112], nt, precision=HI,
                               preferred_element_type=jnp.float32)
    out[...] = acc


def factor(gram, proj):
    vm = pl.BlockSpec(memory_space=pltpu.VMEM)
    return pl.pallas_call(
        factor_kernel,
        out_shape=[jax.ShapeDtypeStruct((448, 448), jnp.float32), jax.ShapeDtypeStruct((ROWS, 112), jnp.float32)],
        in_specs=[vm, vm],
        out_specs=[vm, vm],
        scratch_shapes=[pltpu.VMEM((448, 448), jnp.float32)],
        compiler_params=pltpu.CompilerParams(vmem_limit_bytes=40 * MIB),
        name="factor",
    )(gram, proj)


def shard_rows(block, core):
    rows = jnp.pad(block, ((0, 0), (0, 1), (0, 16))).reshape(7, 2, HALF).transpose(1, 0, 2)
    return jnp.where(core == 0, jnp.pad(rows, ((0, 0), (0, 9), (0, 0))), jnp.pad(rows, ((0, 0), (7, 2), (0, 0))))


def on_device(left_edge, corner, right_edge, single_layer, warm_basis):
    core = lax.axis_index("wide") % 2
    right = shard_rows(right_edge, core)
    warm = shard_rows(warm_basis.transpose(2, 0, 1), core)
    left = left_edge.reshape(7, 7, 7, 112).transpose(0, 2, 1, 3)
    left = jnp.pad(left, ((0, 0), (0, 0), (0, 1), (0, 16))).reshape(392, 128)
    left = jnp.pad(left, ((0, 8), (0, 0)))
    corner = jnp.pad(corner.reshape(112, 32, 14), ((0, 16), (0, 0), (0, 2))).reshape(128, 512)
    proj, gram = gathers(right, warm, left, corner, single_layer.reshape(2, 49, 49))
    r_factor, rows = factor(gram.reshape(4, 512, 128), proj)
    new_basis = rows[:392].reshape(7, 7, 8, 112)[:, :, :7].reshape(7, 49, 112)
    return new_basis, r_factor


def solution(mesh):
    placed = (
        P("wide", None, "narrow"),
        P("narrow", None),
        P("wide", None, "narrow"),
        P(),
        P(None, "narrow", "wide"),
    )
    return jax.shard_map(
        on_device,
        mesh=mesh,
        in_specs=placed,
        out_specs=(P("wide", None, "narrow"), P()),
        check_vma=False,
    )
```

```python
import functools

import jax
import jax.numpy as jnp
from jax import lax
from jax.experimental import pallas as pl
from jax.experimental.pallas import tpu as pltpu
from jax.sharding import PartitionSpec as P

BOND = 7
BLOCK = 64
SLOT = 16
HALF = 3200
A_LANES = 1280
ROWS = 400
HI = lax.Precision.HIGHEST
MESH = pl.DeviceIdType.MESH
MIB = 1 << 20


def place():
    wide = lax.axis_index("wide")
    core = lax.rem(wide, 2)
    z = lax.rem(lax.div(wide, 2), 8)
    y = lax.div(wide, 16)
    return y, z, core, lax.axis_index("narrow")


def wide_of(y, z, core):
    return (y * 8 + z) * 2 + core


def greet(peers):
    barrier = pltpu.get_barrier_semaphore()
    for peer in peers:
        pl.semaphore_signal(barrier, inc=1, device_id=peer, device_id_type=MESH)
    pl.semaphore_wait(barrier, len(peers))


def gather_kernel(right, warm, left, corner, layer, proj, gram,
                  right_all, warm_all, left_all, corner_all, half, strip, layered, total, ket, bra,
                  paired, merged, part, got, slab, got1, piece, got2,
                  pair_s, pair_r, own_s, ring_r, ring_s, part_s, part_r, x_s, x_r,
                  n_s, n_r, p_s, p_r, a_s, a_r, b_s, b_r, c_s, c_r, d_s, d_r, f_s, f_r):
    y, z, core, x = place()
    zdir = 1 - 2 * core

    def zmove(k):
        return lax.rem(z + 8 + k * zdir, 8)

    def ymove(k):
        return lax.rem(y + 4 + k * zdir, 4)

    def at(yy, zz, cc=None):
        return (wide_of(yy, zz, core if cc is None else cc), x)

    partner = at(y, z, 1 - core)
    others = [(lax.rem(y + k // 2, 4), lax.rem(core + k % 2, 2)) for k in range(1, 8)]
    xs = [lax.rem(x + d, 4) for d in (1, 2, 3)]
    zs = [lax.rem(z + d, 8) for d in range(1, 8)]
    me = wide_of(y, z, core)
    plane = [(lax.rem(x + k // 4, 4), lax.rem(y + k % 4, 4)) for k in (10, 2, 8, 6, 14, 9, 11, 1, 3, 4, 12, 5, 7, 13, 15)]
    greet([at(yy, z, cc) for yy, cc in others] + [at(y, zz) for zz in zs]
          + [(wide_of(lax.rem(y + k % 4, 4), z, core), lax.rem(x + k // 4, 4)) for k in range(4, 16)])

    def push(src, dst, ss, rs, device):
        c = pltpu.make_async_remote_copy(src_ref=src, dst_ref=dst, send_sem=ss, recv_sem=rs,
                                         device_id=device, device_id_type=MESH)
        c.start()

    arrays = ((right, right_all), (warm, warm_all))
    pairs = []
    for g, (src, _) in enumerate(arrays):
        c = pltpu.make_async_remote_copy(src_ref=src.at[1 - core], dst_ref=paired.at[g], send_sem=pair_s.at[g],
                                         recv_sem=pair_r.at[g], device_id=partner, device_id_type=MESH)
        c.start()
        pairs.append(c)
    xcopies = []
    for src, dst, k in ((left, left_all, 0), (corner, corner_all, 1)):
        for d in (1, 2, 3):
            c = pltpu.make_async_remote_copy(
                src_ref=src, dst_ref=dst.at[x], send_sem=x_s.at[k, d - 1], recv_sem=x_r.at[k, d - 1],
                device_id=(wide_of(y, z, core), lax.rem(x + d, 4)), device_id_type=MESH)
            c.start()
            xcopies.append(c)
    own_x = []
    for src, dst, k in ((left, left_all, 0), (corner, corner_all, 1)):
        c = pltpu.make_async_copy(src, dst.at[x], own_s.at[2 + k])
        c.start()
        own_x.append(c)

    bounds = ((0, A_LANES), (A_LANES, HALF))

    def view(g, half, part, yy, zz):
        lo, hi = bounds[part]
        rows = pl.ds(pl.multiple_of((yy * 8 + zz) * SLOT, SLOT), SLOT)
        return arrays[g][1].at[half, rows, lo:hi]

    def slot(yy, zz):
        return yy * 8 + zz

    def send(g, part, yy, zz, device, src=None):
        v = view(g, core, part, yy, zz)
        push(v if src is None else src, v, ring_s.at[g], ring_r.at[g, part, slot(yy, zz)], device)

    def forward_partner(g, part, yy, zz, src=None):
        v = view(g, core, part, yy, zz)
        push(v if src is None else src, v, part_s.at[g], part_r.at[g], partner)

    def arrived(g, part, yy, zz):
        v = view(g, core, part, yy, zz)
        pltpu.make_async_copy(v, v, ring_r.at[g, part, slot(yy, zz)]).wait()

    own_copies = []
    znext, zprev = at(y, zmove(1)), at(y, zmove(-1))
    ynext, yprev = at(ymove(1), z), at(ymove(-1), z)

    def begin(g):
        pairs[g].wait()
        merged[g] = paired[g] + arrays[g][0][core]
        c = pltpu.make_async_copy(
            merged.at[g], arrays[g][1].at[core, pl.ds(pl.multiple_of((y * 8 + z) * SLOT, SLOT), SLOT), :], own_s.at[g])
        c.start()
        own_copies.append(c)
        a, b = merged.at[g, :, 0:A_LANES], merged.at[g, :, A_LANES:HALF]
        va = view(g, core, 0, y, z)
        for d in (1, 2, 3):
            push(a, va, ring_s.at[g], ring_r.at[g, 0, slot(y, z)], at(ymove(d), z))
        send(g, 1, y, z, znext, b)
        send(g, 1, y, z, zprev, b)
        send(g, 0, y, z, znext, a)
        send(g, 0, y, z, zprev, a)
        send(g, 1, y, z, ynext, b)
        send(g, 1, y, z, yprev, b)
        forward_partner(g, 0, y, z, a)
        forward_partner(g, 1, y, z, b)

    def column(g):
        for d in (1, 2, 3):
            yy = ymove(d)
            arrived(g, 0, yy, z)
            send(g, 0, yy, z, znext)
            send(g, 0, yy, z, zprev)
            forward_partner(g, 0, yy, z)

    def b_ring(g, s, way):
        zz = zmove(-s) if way > 0 else zmove(s)
        arrived(g, 1, y, zz)
        if way > 0 and s < 4:
            send(g, 1, y, zz, znext)
        if way < 0 and s < 3:
            send(g, 1, y, zz, zprev)
        send(g, 1, y, zz, ynext)
        send(g, 1, y, zz, yprev)
        forward_partner(g, 1, y, zz)

    def a_ring(g, s, way, d):
        zz = zmove(-s) if way > 0 else zmove(s)
        yy = ymove(d)
        arrived(g, 0, yy, zz)
        if way > 0 and s < 4:
            send(g, 0, yy, zz, znext)
        if way < 0 and s < 3:
            send(g, 0, yy, zz, zprev)
        forward_partner(g, 0, yy, zz)

    def y_pass(g, zz):
        arrived(g, 1, ymove(-1), zz)
        send(g, 1, ymove(-1), zz, ynext)
        forward_partner(g, 1, ymove(-1), zz)
        arrived(g, 1, ymove(1), zz)
        forward_partner(g, 1, ymove(1), zz)

    def y_last(g, zz):
        arrived(g, 1, ymove(2), zz)
        forward_partner(g, 1, ymove(2), zz)

    def ring_steps(g):
        steps = [lambda: y_pass(g, z)]
        for k in (1, 2, 3, 4):
            for way in (1, -1):
                if way < 0 and k == 4:
                    continue
                steps.append(functools.partial(b_ring, g, k, way))
                steps.extend(functools.partial(a_ring, g, k, way, d) for d in range(4))
            if k > 1:
                steps.append(functools.partial(y_pass, g, zmove(-(k - 1))))
                steps.append(functools.partial(y_pass, g, zmove(k - 1)))
        steps.append(lambda: y_pass(g, zmove(-4)))
        steps.extend(functools.partial(y_last, g, zmove(k)) for k in range(8))
        return steps

    def from_partner(g):
        settle(arrays[g][1].at[1 - core], part_r.at[g])

    def settle(ref, sem):
        pltpu.make_async_copy(ref, ref, sem).wait()

    begin(0)
    weights(layer, ket, bra)
    column(0)
    steps = ring_steps(0)
    for step in steps[:-17]:
        step()
    begin(1)
    for step in steps[-17:]:
        step()
    column(1)
    for c in xcopies + own_x:
        c.wait()
    acc = jnp.zeros((ROWS, 512), jnp.float32)
    for n in range(4):
        acc += jnp.dot(left_all[n], corner_all[n], preferred_element_type=jnp.float32)
    half[...] = acc.astype(jnp.bfloat16)
    own_copies[0].wait()
    from_partner(0)

    work = compute_steps(half, right_all, ket, bra, strip, layered)
    steps = ring_steps(1)
    done = 0
    for k, compute in enumerate(work):
        compute()
        upto = len(steps) * (k + 1) // len(work)
        for step in steps[done:upto]:
            step()
        done = upto
    own_copies[1].wait()
    from_partner(1)

    def start(src, dst, ss, rs, device):
        c = pltpu.make_async_remote_copy(src_ref=src, dst_ref=dst, send_sem=ss, recv_sem=rs,
                                         device_id=device, device_id_type=MESH)
        c.start()
        return c

    c1 = [None] * 3
    for pair in ((1, 0), (2, None)):
        names = [x if d is None else xs[d] for d in pair]
        project(strip, warm_all, total, part, names)
        for d in pair:
            if d is not None:
                c1[d] = start(part.at[xs[d]], got.at[d], n_s.at[d], n_r.at[d], (me, xs[d]))
    acc = part[x].astype(jnp.float32)
    for d in range(3):
        c1[d].wait_recv()
        acc += got[d].astype(jnp.float32)
    proj[x] = acc.astype(jnp.bfloat16)
    c2 = [start(proj.at[x], proj.at[x], p_s.at[d], p_r.at[d], (me, xs[d])) for d in range(3)]
    own = acc.astype(jnp.bfloat16)
    tn = (((0,), (0,)), ((), ()))
    scale = 1.0 / (448 * 49)

    def product(n):
        slab[pl.ds(pl.multiple_of(n * 128, 128), 128), :] = lax.dot_general(
            proj[n], own, tn, preferred_element_type=jnp.float32) * scale

    product(x)
    for d in (0, 2, 1):
        c2[d].wait_recv()
        product(lax.rem(x + 3 - d, 4))

    def rows(k, size):
        return pl.ds(pl.multiple_of(k * size, size), size)

    mine = y * 2 + core
    c3 = [start(slab.at[rows(yy * 2 + cc, 64)], got1.at[k], a_s.at[k], a_r.at[k], (wide_of(yy, z, cc), x))
          for k, (yy, cc) in enumerate(others)]
    acc = slab[rows(mine, 64), :]
    for k in range(7):
        c3[k].wait_recv()
        acc += got1[k]
    piece[...] = acc
    c4 = [start(piece.at[rows(zz, 8)], got2.at[k], b_s.at[k], b_r.at[k], (wide_of(y, zz, core), x))
          for k, zz in enumerate(zs)]
    acc = piece[rows(z, 8), :]
    for k in range(7):
        c4[k].wait_recv()
        acc += got2[k]
    spot = gram.at[x, y, core, rows(z, 8)]
    gram[x, y, core, rows(z, 8), :] = acc
    c5 = [start(spot, spot, c_s.at[k], c_r.at[k], at(y, zz)) for k, zz in enumerate(zs)]
    for c in c5:
        c.wait_recv()
    spot = gram.at[x, y, core]
    c6 = [start(spot, spot, d_s.at[k], d_r.at[k], (wide_of(yy, z, core), xx)) for k, (xx, yy) in enumerate(plane)]
    start(spot, spot, f_s, f_r, partner)
    for k in (7, 8, 9, 10, 2, 1, 11, 12, 13, 14, 3, 4, 5, 6, 0):
        xx, yy = plane[k]
        c6[k].wait_recv()
        spot = gram.at[lax.rem(2 * x + 4 - xx, 4), lax.rem(2 * y + 4 - yy, 4), core]
        start(spot, spot, f_s, f_r, partner)
    settle(gram.at[:, :, core], f_s)
    settle(gram.at[:, :, 1 - core], f_r)
    for c in c1 + c2 + c3 + c4 + c5 + c6:
        c.wait_send()
    for g in (0, 1):
        settle(arrays[g][1].at[core], part_s.at[g])
        settle(arrays[g][1].at[core, 0:496], ring_s.at[g])


def iota(shape, axis):
    return lax.broadcasted_iota(jnp.int32, shape, axis)


def flags(mask):
    return jnp.where(mask, 1.0, 0.0).astype(jnp.bfloat16)


def mm(a, b):
    return jnp.dot(a, b, preferred_element_type=jnp.float32).astype(jnp.bfloat16)


def mm_nt(a, b):
    return lax.dot_general(a, b, (((1,), (1,)), ((), ())), preferred_element_type=jnp.float32).astype(jnp.bfloat16)


def weights(layer, ket, bra):
    row, col = iota((784, 49), 0), iota((784, 49), 1)
    low = row & 15
    spread = mm_nt(flags((row >> 4 == col) & (low < 7)), layer[0])
    spread += mm_nt(flags((row >> 4 == col) & (low >= 7) & (low < 14)), layer[1])
    row, col = iota((49, ROWS), 0), iota((49, ROWS), 1)
    q, u = col >> 3, col & 7
    full = mm(spread, flags((u < 7) & (q < 49) & (row == u * 7 + ((q * 37) >> 8))))
    row, col = iota((784, ROWS), 0), iota((784, ROWS), 1)
    low, q = row & 15, col >> 3
    same = jnp.where(low < 7, low, low - 7) == q - 7 * ((q * 37) >> 8)
    ket[...] = jnp.where(same, full.astype(jnp.float32), 0.0).astype(jnp.bfloat16)
    row, col = iota((56, 49), 0), iota((56, 49), 1)
    lead = flags((row & 7 < 7) & (col == (row & 7) * 7 + (row >> 3)))
    row, col = iota((49, 112), 0), iota((49, 112), 1)
    low = col & 15
    acc = jnp.zeros((56, 112), jnp.float32)
    for s in range(2):
        ok = (low >= 7 * s) & (low < 7 * s + 7) & (row == (col >> 4) * 7 + low - 7 * s)
        acc += mm(mm_nt(lead, layer[s]), flags(ok)).astype(jnp.float32)
    bra[...] = acc.astype(jnp.bfloat16)


def compute_steps(half, right, ket, bra, strip, layered):
    def strips(h, chunk):
        res = jnp.dot(half[...], right[h, :, chunk * 640:(chunk + 1) * 640], preferred_element_type=jnp.float32)
        for j in range(5):
            first = (h * 25 + chunk * 5 + j) * 8
            strip[:, first:first + 8, :] = res[:, j * 128:(j + 1) * 128].reshape(50, 8, 128)

    def kets(first):
        @pl.loop(first, first + 5)
        def _(t):
            x = jnp.concatenate([strip[2 * t].astype(jnp.bfloat16), strip[2 * t + 1].astype(jnp.bfloat16)], axis=1)
            res = jnp.dot(ket[...], x, preferred_element_type=jnp.float32).astype(jnp.bfloat16)
            for j in range(2):
                rows = pl.ds(pl.multiple_of((2 * t + j) * 16, 16), 16)
                layered[:, rows, :] = res[:, j * 128:(j + 1) * 128].reshape(49, 16, 128)

    def clear():
        strip[49] = jnp.zeros((ROWS, 128), jnp.float32)
        strip[:, 392:400, :] = jnp.zeros((50, 8, 128), jnp.float32)

    def bras(d):
        @pl.loop(0, 7)
        def _(r):
            x = jnp.concatenate([layered[d * 7 + r, i * 112:(i + 1) * 112, :] for i in range(7)], axis=1)
            res = jnp.dot(bra[...], x, preferred_element_type=jnp.float32)
            for i in range(7):
                for s in range(7):
                    strip[r * 7 + s, (i * 7 + d) * 8:(i * 7 + d) * 8 + 8, :] = (
                        res[s * 8:(s + 1) * 8, i * 128:(i + 1) * 128])

    work = [functools.partial(strips, h, chunk) for h in range(2) for chunk in range(5)]
    work += [functools.partial(kets, 5 * t) for t in range(5)]
    work += [clear]
    work += [functools.partial(bras, d) for d in range(7)]
    return work


def project(enlarged, warm, total, part, names):
    total[...] = jnp.zeros_like(total)
    spans = [pl.ds(pl.multiple_of(n * 128, 128), 128) for n in names]
    for h in range(2):
        @pl.loop(0, 5)
        def _(chunk):
            cols = pl.ds(pl.multiple_of(chunk * 640, 640), 640)
            x = jnp.concatenate(
                [enlarged[h * 25 + chunk * 5 + j].astype(jnp.bfloat16) for j in range(5)], axis=1)
            w = jnp.concatenate([warm[h, span, cols] for span in spans], axis=0)
            total[...] += lax.dot_general(x, w, (((1,), (1,)), ((), ())), preferred_element_type=jnp.float32)
    row, col = iota((128, 128), 0), iota((128, 128), 1)
    pick = flags((row & 15 < 14) & (col == (row >> 4) * 14 + (row & 15)))
    for k, n in enumerate(names):
        part[n] = mm(total[:, k * 128:(k + 1) * 128].astype(jnp.bfloat16), pick)


def gathers(right, warm, left, corner, layer):
    dma = pltpu.SemaphoreType.DMA
    vm = pl.BlockSpec(memory_space=pltpu.VMEM)
    return pl.pallas_call(
        gather_kernel,
        out_shape=[
            jax.ShapeDtypeStruct((4, ROWS, 128), jnp.bfloat16),
            jax.ShapeDtypeStruct((4, 4, 2, 64, 128), jnp.float32),
        ],
        in_specs=[vm] * 5,
        out_specs=[vm, vm],
        scratch_shapes=[
            pltpu.VMEM((2, 32 * SLOT, HALF), jnp.bfloat16),
            pltpu.VMEM((2, 32 * SLOT, HALF), jnp.bfloat16),
            pltpu.VMEM((4, ROWS, 128), jnp.bfloat16),
            pltpu.VMEM((4, 128, 512), jnp.bfloat16),
            pltpu.VMEM((ROWS, 512), jnp.bfloat16),
            pltpu.VMEM((50, ROWS, 128), jnp.float32),
            pltpu.VMEM((49, 800, 128), jnp.bfloat16),
            pltpu.VMEM((ROWS, 256), jnp.float32),
            pltpu.VMEM((784, ROWS), jnp.bfloat16),
            pltpu.VMEM((56, 112), jnp.bfloat16),
            pltpu.VMEM((2, SLOT, HALF), jnp.bfloat16),
            pltpu.VMEM((2, SLOT, HALF), jnp.bfloat16),
            pltpu.VMEM((4, ROWS, 128), jnp.bfloat16),
            pltpu.VMEM((3, ROWS, 128), jnp.bfloat16),
            pltpu.VMEM((512, 128), jnp.float32),
            pltpu.VMEM((7, 64, 128), jnp.float32),
            pltpu.VMEM((64, 128), jnp.float32),
            pltpu.VMEM((7, 8, 128), jnp.float32),
            dma((2,)), dma((2,)), dma((4,)), dma((2, 2, 32)), dma((2,)), dma((2,)), dma((2,)), dma((2, 3)), dma((2, 3)),
            dma((3,)), dma((3,)), dma((3,)), dma((3,)), dma((7,)), dma((7,)), dma((7,)), dma((7,)),
            dma((7,)), dma((7,)), dma((15,)), dma((15,)), dma, dma,
        ],
        compiler_params=pltpu.CompilerParams(collective_id=1, has_side_effects=True, vmem_limit_bytes=60 * MIB),
        name="gathers",
    )(right, warm, left, corner, layer)


def eliminate(diag):
    n = BLOCK
    row_id, col_id = iota((n, n), 0), iota((n, n), 1)
    wide = jnp.concatenate([diag, jnp.where(row_id == col_id, 1.0, 0.0).astype(jnp.float32)], axis=1)
    groups = [wide[8 * g:8 * g + 8] for g in range(n // 8)]
    sub = iota((8, 2 * n), 0)

    def full(v):
        return jnp.broadcast_to(v, (8, 2 * n))

    for g in range(n // 8):
        k, own = 8 * g, groups[g]
        rows = [full(own[i:i + 1, :]) for i in range(8)]
        cols = [full(own[:, k + j:k + j + 1]) for j in range(8)]
        e = {(i, j): full(cols[j][i:i + 1, :]) for i in range(8) for j in range(i, 8)}
        scaled, s = [], {}
        for r in range(8):
            inv = 1.0 / e[r, r]
            scaled.append(rows[r] * inv)
            for j in range(r + 1, 8):
                s[r, j] = e[r, j] * inv
            for i in range(r + 1, 8):
                rows[i] = rows[i] - e[r, i] * scaled[r]
                for j in range(i, 8):
                    e[i, j] = e[i, j] - e[r, i] * s[r, j]
        for h in range(g + 1, n // 8):
            below = groups[h]
            c = [full(below[:, k + j:k + j + 1]) for j in range(8)]
            for r in range(8):
                below = below - c[r] * scaled[r]
                for j in range(r + 1, 8):
                    c[j] = c[j] - c[r] * s[r, j]
            groups[h] = below
        for i in range(1, 8):
            own = jnp.where(sub == i, rows[i], own)
        groups[g] = own
    wide = jnp.concatenate(groups, axis=0)
    upper, lower = wide[:, :n], wide[:, n:]
    d = jnp.sum(jnp.where(row_id == col_id, upper, 0.0), axis=1, keepdims=True)
    root = lax.rsqrt(d)
    root = root * (1.5 - 0.5 * d * root * root)
    return jnp.where(row_id <= col_id, upper * root, 0.0), jnp.where(row_id >= col_id, lower * root, 0.0)


def factor_kernel(gram, proj, r_ref, out, work):
    n = 448
    x = lax.axis_index("narrow")
    for a in range(4):
        for b in range(4):
            work[a * 112:(a + 1) * 112, b * 112:(b + 1) * 112] = gram[b, a * 128:a * 128 + 112, 0:112]
    r_ref[...] = jnp.zeros_like(r_ref)
    col = lax.broadcasted_iota(jnp.int32, (BLOCK, n), 1)
    row = lax.broadcasted_iota(jnp.int32, (BLOCK, n), 0)
    for b in range(n // BLOCK):
        lo, hi = b * BLOCK, (b + 1) * BLOCK
        r, inverse = eliminate(work[lo:hi, lo:hi])
        inside = (col >= lo) & (col < hi)
        src = jnp.where(inside, jnp.where(col - lo == row, 1.0, 0.0), work[lo:hi, :])
        full = jnp.dot(inverse, src, precision=HI, preferred_element_type=jnp.float32)
        work[lo:hi, :] = jnp.where(col < hi, full, 0.0)
        rest = jnp.where(col >= hi, full, 0.0)
        r_ref[lo:hi, :] = rest
        r_ref[lo:hi, lo:hi] = r
        if hi < n:
            at = lax.broadcasted_iota(jnp.int32, (n - hi, n), 1)
            old = jnp.where((at >= lo) & (at < hi), 0.0, work[hi:, :])
            work[hi:, :] = old - lax.dot_general(rest[:, hi:], full, (((0,), (0,)), ((), ())), precision=HI,
                                                 preferred_element_type=jnp.float32)
    own = work[pl.ds(pl.multiple_of(x * 112, 8), 112), :]
    nt = (((1,), (1,)), ((), ()))
    acc = jnp.zeros((ROWS, 112), jnp.float32)
    for b in range(4):
        acc += lax.dot_general(proj[b][:, 0:112].astype(jnp.float32), own[:, b * 112:(b + 1) * 112], nt, precision=HI,
                               preferred_element_type=jnp.float32)
    out[...] = acc


def factor(gram, proj):
    vm = pl.BlockSpec(memory_space=pltpu.VMEM)
    return pl.pallas_call(
        factor_kernel,
        out_shape=[jax.ShapeDtypeStruct((448, 448), jnp.float32), jax.ShapeDtypeStruct((ROWS, 112), jnp.float32)],
        in_specs=[vm, vm],
        out_specs=[vm, vm],
        scratch_shapes=[pltpu.VMEM((448, 448), jnp.float32)],
        compiler_params=pltpu.CompilerParams(vmem_limit_bytes=40 * MIB),
        name="factor",
    )(gram, proj)


def shard_rows(block, core):
    rows = jnp.pad(block, ((0, 0), (0, 1), (0, 16))).reshape(7, 2, HALF).transpose(1, 0, 2)
    return jnp.where(core == 0, jnp.pad(rows, ((0, 0), (0, 9), (0, 0))), jnp.pad(rows, ((0, 0), (7, 2), (0, 0))))


def on_device(left_edge, corner, right_edge, single_layer, warm_basis):
    core = lax.axis_index("wide") % 2
    right = shard_rows(right_edge, core)
    warm = shard_rows(warm_basis.transpose(2, 0, 1), core)
    left = left_edge.reshape(7, 7, 7, 112).transpose(0, 2, 1, 3)
    left = jnp.pad(left, ((0, 0), (0, 0), (0, 1), (0, 16))).reshape(392, 128)
    left = jnp.pad(left, ((0, 8), (0, 0)))
    corner = jnp.pad(corner.reshape(112, 32, 14), ((0, 16), (0, 0), (0, 2))).reshape(128, 512)
    proj, gram = gathers(right, warm, left, corner, single_layer.reshape(2, 49, 49))
    r_factor, rows = factor(gram.reshape(4, 512, 128), proj)
    new_basis = rows[:392].reshape(7, 7, 8, 112)[:, :, :7].reshape(7, 49, 112)
    return new_basis, r_factor


def solution(mesh):
    placed = (
        P("wide", None, "narrow"),
        P("narrow", None),
        P("wide", None, "narrow"),
        P(),
        P(None, "narrow", "wide"),
    )
    return jax.shard_map(
        on_device,
        mesh=mesh,
        in_specs=placed,
        out_specs=(P("wide", None, "narrow"), P()),
        check_vma=False,
    )
```

```python
import functools

import jax
import jax.numpy as jnp
from jax import lax
from jax.experimental import pallas as pl
from jax.experimental.pallas import tpu as pltpu
from jax.sharding import PartitionSpec as P

BOND = 7
BLOCK = 64
SLOT = 16
HALF = 3200
A_LANES = 1280
ROWS = 400
HI = lax.Precision.HIGHEST
MESH = pl.DeviceIdType.MESH
MIB = 1 << 20


def place():
    wide = lax.axis_index("wide")
    core = lax.rem(wide, 2)
    z = lax.rem(lax.div(wide, 2), 8)
    y = lax.div(wide, 16)
    return y, z, core, lax.axis_index("narrow")


def wide_of(y, z, core):
    return (y * 8 + z) * 2 + core


def greet(peers):
    barrier = pltpu.get_barrier_semaphore()
    for peer in peers:
        pl.semaphore_signal(barrier, inc=1, device_id=peer, device_id_type=MESH)
    pl.semaphore_wait(barrier, len(peers))


def gather_kernel(right, warm, left, corner, layer, proj, gram,
                  right_all, warm_all, left_all, corner_all, half, strip, layered, total, ket, bra,
                  paired, merged, part, got, slab, got1, piece, got2,
                  pair_s, pair_r, own_s, ring_r, ring_s, part_s, part_r, x_s, x_r,
                  n_s, n_r, p_s, p_r, a_s, a_r, b_s, b_r, c_s, c_r, d_s, d_r, f_s, f_r):
    y, z, core, x = place()
    zdir = 1 - 2 * core

    def zmove(k):
        return lax.rem(z + 8 + k * zdir, 8)

    def ymove(k):
        return lax.rem(y + 4 + k * zdir, 4)

    def at(yy, zz, cc=None):
        return (wide_of(yy, zz, core if cc is None else cc), x)

    partner = at(y, z, 1 - core)
    others = [(lax.rem(y + k // 2, 4), lax.rem(core + k % 2, 2)) for k in range(1, 8)]
    xs = [lax.rem(x + d, 4) for d in (1, 2, 3)]
    zs = [lax.rem(z + d, 8) for d in range(1, 8)]
    me = wide_of(y, z, core)
    plane = [(lax.rem(x + k // 4, 4), lax.rem(y + k % 4, 4)) for k in (10, 2, 8, 6, 14, 9, 11, 1, 3, 4, 12, 5, 7, 13, 15)]
    greet([at(yy, z, cc) for yy, cc in others] + [at(y, zz) for zz in zs]
          + [(wide_of(lax.rem(y + k % 4, 4), z, core), lax.rem(x + k // 4, 4)) for k in range(4, 16)])

    def push(src, dst, ss, rs, device):
        c = pltpu.make_async_remote_copy(src_ref=src, dst_ref=dst, send_sem=ss, recv_sem=rs,
                                         device_id=device, device_id_type=MESH)
        c.start()

    arrays = ((right, right_all), (warm, warm_all))
    pairs = []
    for g, (src, _) in enumerate(arrays):
        c = pltpu.make_async_remote_copy(src_ref=src.at[1 - core], dst_ref=paired.at[g], send_sem=pair_s.at[g],
                                         recv_sem=pair_r.at[g], device_id=partner, device_id_type=MESH)
        c.start()
        pairs.append(c)
    xcopies = []
    for src, dst, k in ((left, left_all, 0), (corner, corner_all, 1)):
        for d in (1, 2, 3):
            c = pltpu.make_async_remote_copy(
                src_ref=src, dst_ref=dst.at[x], send_sem=x_s.at[k, d - 1], recv_sem=x_r.at[k, d - 1],
                device_id=(wide_of(y, z, core), lax.rem(x + d, 4)), device_id_type=MESH)
            c.start()
            xcopies.append(c)
    own_x = []
    for src, dst, k in ((left, left_all, 0), (corner, corner_all, 1)):
        c = pltpu.make_async_copy(src, dst.at[x], own_s.at[2 + k])
        c.start()
        own_x.append(c)

    bounds = ((0, A_LANES), (A_LANES, HALF))

    def view(g, half, part, yy, zz):
        lo, hi = bounds[part]
        rows = pl.ds(pl.multiple_of((yy * 8 + zz) * SLOT, SLOT), SLOT)
        return arrays[g][1].at[half, rows, lo:hi]

    def slot(yy, zz):
        return yy * 8 + zz

    def send(g, part, yy, zz, device, src=None):
        v = view(g, core, part, yy, zz)
        push(v if src is None else src, v, ring_s.at[g], ring_r.at[g, part, slot(yy, zz)], device)

    def forward_partner(g, part, yy, zz, src=None):
        v = view(g, core, part, yy, zz)
        push(v if src is None else src, v, part_s.at[g], part_r.at[g], partner)

    def arrived(g, part, yy, zz):
        v = view(g, core, part, yy, zz)
        pltpu.make_async_copy(v, v, ring_r.at[g, part, slot(yy, zz)]).wait()

    own_copies = []
    znext, zprev = at(y, zmove(1)), at(y, zmove(-1))
    ynext, yprev = at(ymove(1), z), at(ymove(-1), z)

    def begin(g):
        pairs[g].wait()
        merged[g] = paired[g] + arrays[g][0][core]
        c = pltpu.make_async_copy(
            merged.at[g], arrays[g][1].at[core, pl.ds(pl.multiple_of((y * 8 + z) * SLOT, SLOT), SLOT), :], own_s.at[g])
        c.start()
        own_copies.append(c)
        a, b = merged.at[g, :, 0:A_LANES], merged.at[g, :, A_LANES:HALF]
        va = view(g, core, 0, y, z)
        for d in (1, 2, 3):
            push(a, va, ring_s.at[g], ring_r.at[g, 0, slot(y, z)], at(ymove(d), z))
        send(g, 1, y, z, znext, b)
        send(g, 1, y, z, zprev, b)
        send(g, 0, y, z, znext, a)
        send(g, 0, y, z, zprev, a)
        send(g, 1, y, z, ynext, b)
        send(g, 1, y, z, yprev, b)
        forward_partner(g, 0, y, z, a)
        forward_partner(g, 1, y, z, b)

    def column(g, d):
        yy = ymove(d)
        arrived(g, 0, yy, z)
        send(g, 0, yy, z, znext)
        send(g, 0, yy, z, zprev)
        forward_partner(g, 0, yy, z)

    def b_ring(g, s, way):
        zz = zmove(-s) if way > 0 else zmove(s)
        arrived(g, 1, y, zz)
        if way > 0 and s < 4:
            send(g, 1, y, zz, znext)
        if way < 0 and s < 3:
            send(g, 1, y, zz, zprev)
        send(g, 1, y, zz, ynext)
        send(g, 1, y, zz, yprev)
        forward_partner(g, 1, y, zz)

    def a_ring(g, s, way, d):
        zz = zmove(-s) if way > 0 else zmove(s)
        yy = ymove(d)
        arrived(g, 0, yy, zz)
        if way > 0 and s < 4:
            send(g, 0, yy, zz, znext)
        if way < 0 and s < 3:
            send(g, 0, yy, zz, zprev)
        forward_partner(g, 0, yy, zz)

    def y_pass(g, zz):
        arrived(g, 1, ymove(-1), zz)
        send(g, 1, ymove(-1), zz, ynext)
        forward_partner(g, 1, ymove(-1), zz)
        arrived(g, 1, ymove(1), zz)
        forward_partner(g, 1, ymove(1), zz)

    def y_last(g, zz):
        arrived(g, 1, ymove(2), zz)
        forward_partner(g, 1, ymove(2), zz)

    def ring_steps(g):
        steps = []

        def b_hop(k):
            steps.append(functools.partial(b_ring, g, k, 1))
            if k < 4:
                steps.append(functools.partial(b_ring, g, k, -1))

        def a_hop(k):
            for d in range(4):
                steps.append(functools.partial(a_ring, g, k, 1, d))
                if k < 4:
                    steps.append(functools.partial(a_ring, g, k, -1, d))

        def y_hop(k):
            steps.append(functools.partial(y_pass, g, zmove(-k)))
            if 0 < k < 4:
                steps.append(functools.partial(y_pass, g, zmove(k)))

        def y_end(*ks):
            steps.extend(functools.partial(y_last, g, zmove(k)) for k in ks)

        b_hop(1)
        steps.extend(functools.partial(column, g, d) for d in (1, 3, 2))
        y_hop(0)
        b_hop(2)
        y_hop(1)
        a_hop(1)
        b_hop(3)
        y_hop(2)
        b_hop(4)
        y_end(0)
        a_hop(2)
        y_hop(3)
        y_end(-1, 1)
        y_hop(4)
        y_end(-2, 2)
        a_hop(3)
        y_end(-3, 3, 4)
        a_hop(4)
        return steps

    def from_partner(g):
        settle(arrays[g][1].at[1 - core], part_r.at[g])

    def settle(ref, sem):
        pltpu.make_async_copy(ref, ref, sem).wait()

    begin(0)
    weights(layer, ket, bra)
    steps = ring_steps(0)
    for step in steps[:-8]:
        step()
    for c in xcopies + own_x:
        c.wait()
    acc = jnp.zeros((ROWS, 512), jnp.float32)
    for n in range(4):
        acc += jnp.dot(left_all[n], corner_all[n], preferred_element_type=jnp.float32)
    half[...] = acc.astype(jnp.bfloat16)
    begin(1)
    for step in steps[-8:]:
        step()
    own_copies[0].wait()
    from_partner(0)

    work = compute_steps(half, right_all, ket, bra, strip, layered)
    steps = ring_steps(1)
    done = 0
    for k, compute in enumerate(work):
        compute()
        upto = int(len(steps) * ((k + 1) / len(work)) ** 1.5)
        for step in steps[done:upto]:
            step()
        done = upto
    own_copies[1].wait()
    from_partner(1)

    def start(src, dst, ss, rs, device):
        c = pltpu.make_async_remote_copy(src_ref=src, dst_ref=dst, send_sem=ss, recv_sem=rs,
                                         device_id=device, device_id_type=MESH)
        c.start()
        return c

    c1 = [None] * 3
    for pair in ((1, 0), (2, None)):
        names = [x if d is None else xs[d] for d in pair]
        project(strip, warm_all, total, part, names)
        for d in pair:
            if d is not None:
                c1[d] = start(part.at[xs[d]], got.at[d], n_s.at[d], n_r.at[d], (me, xs[d]))
    acc = part[x].astype(jnp.float32)
    for d in range(3):
        c1[d].wait_recv()
        acc += got[d].astype(jnp.float32)
    proj[x] = acc.astype(jnp.bfloat16)
    c2 = [start(proj.at[x], proj.at[x], p_s.at[d], p_r.at[d], (me, xs[d])) for d in range(3)]
    own = acc.astype(jnp.bfloat16)
    tn = (((0,), (0,)), ((), ()))
    scale = 1.0 / (448 * 49)

    def product(n):
        slab[pl.ds(pl.multiple_of(n * 128, 128), 128), :] = lax.dot_general(
            proj[n], own, tn, preferred_element_type=jnp.float32) * scale

    product(x)
    for d in (0, 2, 1):
        c2[d].wait_recv()
        product(lax.rem(x + 3 - d, 4))

    def rows(k, size):
        return pl.ds(pl.multiple_of(k * size, size), size)

    mine = y * 2 + core
    c3 = [start(slab.at[rows(yy * 2 + cc, 64)], got1.at[k], a_s.at[k], a_r.at[k], (wide_of(yy, z, cc), x))
          for k, (yy, cc) in enumerate(others)]
    acc = slab[rows(mine, 64), :]
    for k in range(7):
        c3[k].wait_recv()
        acc += got1[k]
    piece[...] = acc
    c4 = [start(piece.at[rows(zz, 8)], got2.at[k], b_s.at[k], b_r.at[k], (wide_of(y, zz, core), x))
          for k, zz in enumerate(zs)]
    acc = piece[rows(z, 8), :]
    for k in range(7):
        c4[k].wait_recv()
        acc += got2[k]
    spot = gram.at[x, y, core, rows(z, 8)]
    gram[x, y, core, rows(z, 8), :] = acc
    c5 = [start(spot, spot, c_s.at[k], c_r.at[k], at(y, zz)) for k, zz in enumerate(zs)]
    for c in c5:
        c.wait_recv()
    spot = gram.at[x, y, core]
    c6 = [start(spot, spot, d_s.at[k], d_r.at[k], (wide_of(yy, z, core), xx)) for k, (xx, yy) in enumerate(plane)]
    start(spot, spot, f_s, f_r, partner)
    for k in (7, 8, 9, 10, 2, 1, 11, 12, 13, 14, 3, 4, 5, 6, 0):
        xx, yy = plane[k]
        c6[k].wait_recv()
        spot = gram.at[lax.rem(2 * x + 4 - xx, 4), lax.rem(2 * y + 4 - yy, 4), core]
        start(spot, spot, f_s, f_r, partner)
    settle(gram.at[:, :, core], f_s)
    settle(gram.at[:, :, 1 - core], f_r)
    for c in c1 + c2 + c3 + c4 + c5 + c6:
        c.wait_send()
    for g in (0, 1):
        settle(arrays[g][1].at[core], part_s.at[g])
        settle(arrays[g][1].at[core, 0:496], ring_s.at[g])


def iota(shape, axis):
    return lax.broadcasted_iota(jnp.int32, shape, axis)


def flags(mask):
    return jnp.where(mask, 1.0, 0.0).astype(jnp.bfloat16)


def mm(a, b):
    return jnp.dot(a, b, preferred_element_type=jnp.float32).astype(jnp.bfloat16)


def mm_nt(a, b):
    return lax.dot_general(a, b, (((1,), (1,)), ((), ())), preferred_element_type=jnp.float32).astype(jnp.bfloat16)


def weights(layer, ket, bra):
    row, col = iota((784, 49), 0), iota((784, 49), 1)
    low = row & 15
    spread = mm_nt(flags((row >> 4 == col) & (low < 7)), layer[0])
    spread += mm_nt(flags((row >> 4 == col) & (low >= 7) & (low < 14)), layer[1])
    row, col = iota((49, ROWS), 0), iota((49, ROWS), 1)
    q, u = col >> 3, col & 7
    full = mm(spread, flags((u < 7) & (q < 49) & (row == u * 7 + ((q * 37) >> 8))))
    row, col = iota((784, ROWS), 0), iota((784, ROWS), 1)
    low, q = row & 15, col >> 3
    same = jnp.where(low < 7, low, low - 7) == q - 7 * ((q * 37) >> 8)
    ket[...] = jnp.where(same, full.astype(jnp.float32), 0.0).astype(jnp.bfloat16)
    row, col = iota((56, 49), 0), iota((56, 49), 1)
    lead = flags((row & 7 < 7) & (col == (row & 7) * 7 + (row >> 3)))
    row, col = iota((49, 112), 0), iota((49, 112), 1)
    low = col & 15
    acc = jnp.zeros((56, 112), jnp.float32)
    for s in range(2):
        ok = (low >= 7 * s) & (low < 7 * s + 7) & (row == (col >> 4) * 7 + low - 7 * s)
        acc += mm(mm_nt(lead, layer[s]), flags(ok)).astype(jnp.float32)
    bra[...] = acc.astype(jnp.bfloat16)


def compute_steps(half, right, ket, bra, strip, layered):
    def strips(h, chunk):
        res = jnp.dot(half[...], right[h, :, chunk * 640:(chunk + 1) * 640], preferred_element_type=jnp.float32)
        for j in range(5):
            first = (h * 25 + chunk * 5 + j) * 8
            strip[:, first:first + 8, :] = res[:, j * 128:(j + 1) * 128].reshape(50, 8, 128)

    def kets(first):
        @pl.loop(first, first + 5)
        def _(t):
            x = jnp.concatenate([strip[2 * t].astype(jnp.bfloat16), strip[2 * t + 1].astype(jnp.bfloat16)], axis=1)
            res = jnp.dot(ket[...], x, preferred_element_type=jnp.float32).astype(jnp.bfloat16)
            for j in range(2):
                rows = pl.ds(pl.multiple_of((2 * t + j) * 16, 16), 16)
                layered[:, rows, :] = res[:, j * 128:(j + 1) * 128].reshape(49, 16, 128)

    def clear():
        strip[49] = jnp.zeros((ROWS, 128), jnp.float32)
        strip[:, 392:400, :] = jnp.zeros((50, 8, 128), jnp.float32)

    def bras(d):
        @pl.loop(0, 7)
        def _(r):
            x = jnp.concatenate([layered[d * 7 + r, i * 112:(i + 1) * 112, :] for i in range(7)], axis=1)
            res = jnp.dot(bra[...], x, preferred_element_type=jnp.float32)
            for i in range(7):
                for s in range(7):
                    strip[r * 7 + s, (i * 7 + d) * 8:(i * 7 + d) * 8 + 8, :] = (
                        res[s * 8:(s + 1) * 8, i * 128:(i + 1) * 128])

    work = [functools.partial(strips, h, chunk) for h in range(2) for chunk in range(5)]
    work += [functools.partial(kets, 5 * t) for t in range(5)]
    work += [clear]
    work += [functools.partial(bras, d) for d in range(7)]
    return work


def project(enlarged, warm, total, part, names):
    total[...] = jnp.zeros_like(total)
    spans = [pl.ds(pl.multiple_of(n * 128, 128), 128) for n in names]
    for h in range(2):
        @pl.loop(0, 5)
        def _(chunk):
            cols = pl.ds(pl.multiple_of(chunk * 640, 640), 640)
            x = jnp.concatenate(
                [enlarged[h * 25 + chunk * 5 + j].astype(jnp.bfloat16) for j in range(5)], axis=1)
            w = jnp.concatenate([warm[h, span, cols] for span in spans], axis=0)
            total[...] += lax.dot_general(x, w, (((1,), (1,)), ((), ())), preferred_element_type=jnp.float32)
    row, col = iota((128, 128), 0), iota((128, 128), 1)
    pick = flags((row & 15 < 14) & (col == (row >> 4) * 14 + (row & 15)))
    for k, n in enumerate(names):
        part[n] = mm(total[:, k * 128:(k + 1) * 128].astype(jnp.bfloat16), pick)


def gathers(right, warm, left, corner, layer):
    dma = pltpu.SemaphoreType.DMA
    vm = pl.BlockSpec(memory_space=pltpu.VMEM)
    return pl.pallas_call(
        gather_kernel,
        out_shape=[
            jax.ShapeDtypeStruct((4, ROWS, 128), jnp.bfloat16),
            jax.ShapeDtypeStruct((4, 4, 2, 64, 128), jnp.float32),
        ],
        in_specs=[vm] * 5,
        out_specs=[vm, vm],
        scratch_shapes=[
            pltpu.VMEM((2, 32 * SLOT, HALF), jnp.bfloat16),
            pltpu.VMEM((2, 32 * SLOT, HALF), jnp.bfloat16),
            pltpu.VMEM((4, ROWS, 128), jnp.bfloat16),
            pltpu.VMEM((4, 128, 512), jnp.bfloat16),
            pltpu.VMEM((ROWS, 512), jnp.bfloat16),
            pltpu.VMEM((50, ROWS, 128), jnp.float32),
            pltpu.VMEM((49, 800, 128), jnp.bfloat16),
            pltpu.VMEM((ROWS, 256), jnp.float32),
            pltpu.VMEM((784, ROWS), jnp.bfloat16),
            pltpu.VMEM((56, 112), jnp.bfloat16),
            pltpu.VMEM((2, SLOT, HALF), jnp.bfloat16),
            pltpu.VMEM((2, SLOT, HALF), jnp.bfloat16),
            pltpu.VMEM((4, ROWS, 128), jnp.bfloat16),
            pltpu.VMEM((3, ROWS, 128), jnp.bfloat16),
            pltpu.VMEM((512, 128), jnp.float32),
            pltpu.VMEM((7, 64, 128), jnp.float32),
            pltpu.VMEM((64, 128), jnp.float32),
            pltpu.VMEM((7, 8, 128), jnp.float32),
            dma((2,)), dma((2,)), dma((4,)), dma((2, 2, 32)), dma((2,)), dma((2,)), dma((2,)), dma((2, 3)), dma((2, 3)),
            dma((3,)), dma((3,)), dma((3,)), dma((3,)), dma((7,)), dma((7,)), dma((7,)), dma((7,)),
            dma((7,)), dma((7,)), dma((15,)), dma((15,)), dma, dma,
        ],
        compiler_params=pltpu.CompilerParams(collective_id=1, has_side_effects=True, vmem_limit_bytes=46 * MIB),
        name="gathers",
    )(right, warm, left, corner, layer)


def eliminate(diag):
    n = BLOCK
    row_id, col_id = iota((n, n), 0), iota((n, n), 1)
    wide = jnp.concatenate([diag, jnp.where(row_id == col_id, 1.0, 0.0).astype(jnp.float32)], axis=1)
    groups = [wide[8 * g:8 * g + 8] for g in range(n // 8)]
    sub = iota((8, 2 * n), 0)

    def full(v):
        return jnp.broadcast_to(v, (8, 2 * n))

    for g in range(n // 8):
        k, own = 8 * g, groups[g]
        rows = [full(own[i:i + 1, :]) for i in range(8)]
        cols = [full(own[:, k + j:k + j + 1]) for j in range(8)]
        e = {(i, j): full(cols[j][i:i + 1, :]) for i in range(8) for j in range(i, 8)}
        scaled, s = [], {}
        for r in range(8):
            inv = 1.0 / e[r, r]
            scaled.append(rows[r] * inv)
            for j in range(r + 1, 8):
                s[r, j] = e[r, j] * inv
            for i in range(r + 1, 8):
                rows[i] = rows[i] - e[r, i] * scaled[r]
                for j in range(i, 8):
                    e[i, j] = e[i, j] - e[r, i] * s[r, j]
        for h in range(g + 1, n // 8):
            below = groups[h]
            c = [full(below[:, k + j:k + j + 1]) for j in range(8)]
            for r in range(8):
                below = below - c[r] * scaled[r]
                for j in range(r + 1, 8):
                    c[j] = c[j] - c[r] * s[r, j]
            groups[h] = below
        for i in range(1, 8):
            own = jnp.where(sub == i, rows[i], own)
        groups[g] = own
    wide = jnp.concatenate(groups, axis=0)
    upper, lower = wide[:, :n], wide[:, n:]
    d = jnp.sum(jnp.where(row_id == col_id, upper, 0.0), axis=1, keepdims=True)
    root = lax.rsqrt(d)
    root = root * (1.5 - 0.5 * d * root * root)
    return jnp.where(row_id <= col_id, upper * root, 0.0), jnp.where(row_id >= col_id, lower * root, 0.0)


def factor_kernel(gram, proj, r_ref, out, work):
    n = 448
    x = lax.axis_index("narrow")
    for a in range(4):
        for b in range(4):
            work[a * 112:(a + 1) * 112, b * 112:(b + 1) * 112] = gram[b, a * 128:a * 128 + 112, 0:112]
    r_ref[...] = jnp.zeros_like(r_ref)
    col = lax.broadcasted_iota(jnp.int32, (BLOCK, n), 1)
    row = lax.broadcasted_iota(jnp.int32, (BLOCK, n), 0)
    for b in range(n // BLOCK):
        lo, hi = b * BLOCK, (b + 1) * BLOCK
        r, inverse = eliminate(work[lo:hi, lo:hi])
        inside = (col >= lo) & (col < hi)
        src = jnp.where(inside, jnp.where(col - lo == row, 1.0, 0.0), work[lo:hi, :])
        full = jnp.dot(inverse, src, precision=HI, preferred_element_type=jnp.float32)
        work[lo:hi, :] = jnp.where(col < hi, full, 0.0)
        rest = jnp.where(col >= hi, full, 0.0)
        r_ref[lo:hi, :] = rest
        r_ref[lo:hi, lo:hi] = r
        if hi < n:
            at = lax.broadcasted_iota(jnp.int32, (n - hi, n), 1)
            old = jnp.where((at >= lo) & (at < hi), 0.0, work[hi:, :])
            work[hi:, :] = old - lax.dot_general(rest[:, hi:], full, (((0,), (0,)), ((), ())), precision=HI,
                                                 preferred_element_type=jnp.float32)
    own = work[pl.ds(pl.multiple_of(x * 112, 8), 112), :]
    nt = (((1,), (1,)), ((), ()))
    acc = jnp.zeros((ROWS, 112), jnp.float32)
    for b in range(4):
        acc += lax.dot_general(proj[b][:, 0:112].astype(jnp.float32), own[:, b * 112:(b + 1) * 112], nt, precision=HI,
                               preferred_element_type=jnp.float32)
    out[...] = acc


def factor(gram, proj):
    vm = pl.BlockSpec(memory_space=pltpu.VMEM)
    return pl.pallas_call(
        factor_kernel,
        out_shape=[jax.ShapeDtypeStruct((448, 448), jnp.float32), jax.ShapeDtypeStruct((ROWS, 112), jnp.float32)],
        in_specs=[vm, vm],
        out_specs=[vm, vm],
        scratch_shapes=[pltpu.VMEM((448, 448), jnp.float32)],
        compiler_params=pltpu.CompilerParams(vmem_limit_bytes=40 * MIB),
        name="factor",
    )(gram, proj)


def shard_rows(block, core):
    rows = jnp.pad(block, ((0, 0), (0, 1), (0, 16))).reshape(7, 2, HALF).transpose(1, 0, 2)
    return jnp.where(core == 0, jnp.pad(rows, ((0, 0), (0, 9), (0, 0))), jnp.pad(rows, ((0, 0), (7, 2), (0, 0))))


def on_device(left_edge, corner, right_edge, single_layer, warm_basis):
    core = lax.axis_index("wide") % 2
    right = shard_rows(right_edge, core)
    warm = shard_rows(warm_basis.transpose(2, 0, 1), core)
    left = left_edge.reshape(7, 7, 7, 112).transpose(0, 2, 1, 3)
    left = jnp.pad(left, ((0, 0), (0, 0), (0, 1), (0, 16))).reshape(392, 128)
    left = jnp.pad(left, ((0, 8), (0, 0)))
    corner = jnp.pad(corner.reshape(112, 32, 14), ((0, 16), (0, 0), (0, 2))).reshape(128, 512)
    proj, gram = gathers(right, warm, left, corner, single_layer.reshape(2, 49, 49))
    r_factor, rows = factor(gram.reshape(4, 512, 128), proj)
    new_basis = rows[:392].reshape(7, 7, 8, 112)[:, :, :7].reshape(7, 49, 112)
    return new_basis, r_factor


def solution(mesh):
    placed = (
        P("wide", None, "narrow"),
        P("narrow", None),
        P("wide", None, "narrow"),
        P(),
        P(None, "narrow", "wide"),
    )
    return jax.shard_map(
        on_device,
        mesh=mesh,
        in_specs=placed,
        out_specs=(P("wide", None, "narrow"), P()),
        check_vma=False,
    )
```

```python
import functools

import jax
import jax.numpy as jnp
from jax import lax
from jax.experimental import pallas as pl
from jax.experimental.pallas import tpu as pltpu
from jax.sharding import PartitionSpec as P

BOND = 7
BLOCK = 64
SLOT = 16
HALF = 3200
A_LANES = 1280
ROWS = 400
HI = lax.Precision.HIGHEST
MESH = pl.DeviceIdType.MESH
MIB = 1 << 20


def place():
    wide = lax.axis_index("wide")
    core = lax.rem(wide, 2)
    z = lax.rem(lax.div(wide, 2), 8)
    y = lax.div(wide, 16)
    return y, z, core, lax.axis_index("narrow")


def wide_of(y, z, core):
    return (y * 8 + z) * 2 + core


def greet(peers):
    barrier = pltpu.get_barrier_semaphore()
    for peer in peers:
        pl.semaphore_signal(barrier, inc=1, device_id=peer, device_id_type=MESH)
    pl.semaphore_wait(barrier, len(peers))


def gather_kernel(right, warm, left, corner, layer, proj, gram,
                  right_all, warm_all, left_all, corner_all, half, strip, layered, total, ket, bra,
                  paired, merged, part, got, slab, got1, piece, got2,
                  pair_s, pair_r, own_s, ring_r, ring_s, part_s, part_r, x_s, x_r,
                  n_s, n_r, p_s, p_r, a_s, a_r, b_s, b_r, c_s, c_r, d_s, d_r, f_s, f_r):
    y, z, core, x = place()
    zdir = 1 - 2 * core

    def zmove(k):
        return lax.rem(z + 8 + k * zdir, 8)

    def ymove(k):
        return lax.rem(y + 4 + k * zdir, 4)

    def at(yy, zz, cc=None):
        return (wide_of(yy, zz, core if cc is None else cc), x)

    partner = at(y, z, 1 - core)
    others = [(lax.rem(y + k // 2, 4), lax.rem(core + k % 2, 2)) for k in range(1, 8)]
    xs = [lax.rem(x + d, 4) for d in (1, 2, 3)]
    zs = [lax.rem(z + d, 8) for d in range(1, 8)]
    me = wide_of(y, z, core)
    plane = [(lax.rem(x + k // 4, 4), lax.rem(y + k % 4, 4)) for k in (10, 2, 8, 6, 14, 9, 11, 1, 3, 4, 12, 5, 7, 13, 15)]
    greet([at(yy, z, cc) for yy, cc in others] + [at(y, zz) for zz in zs]
          + [(wide_of(lax.rem(y + k % 4, 4), z, core), lax.rem(x + k // 4, 4)) for k in range(4, 16)])

    def push(src, dst, ss, rs, device):
        c = pltpu.make_async_remote_copy(src_ref=src, dst_ref=dst, send_sem=ss, recv_sem=rs,
                                         device_id=device, device_id_type=MESH)
        c.start()

    arrays = ((right, right_all), (warm, warm_all))
    pairs = []
    for g, (src, _) in enumerate(arrays):
        c = pltpu.make_async_remote_copy(src_ref=src.at[1 - core], dst_ref=paired.at[g], send_sem=pair_s.at[g],
                                         recv_sem=pair_r.at[g], device_id=partner, device_id_type=MESH)
        c.start()
        pairs.append(c)
    xcopies = []
    for src, dst, k in ((left, left_all, 0), (corner, corner_all, 1)):
        for d in (1, 2, 3):
            c = pltpu.make_async_remote_copy(
                src_ref=src, dst_ref=dst.at[x], send_sem=x_s.at[k, d - 1], recv_sem=x_r.at[k, d - 1],
                device_id=(wide_of(y, z, core), lax.rem(x + d, 4)), device_id_type=MESH)
            c.start()
            xcopies.append(c)
    own_x = []
    for src, dst, k in ((left, left_all, 0), (corner, corner_all, 1)):
        c = pltpu.make_async_copy(src, dst.at[x], own_s.at[2 + k])
        c.start()
        own_x.append(c)

    bounds = ((0, A_LANES), (A_LANES, HALF))

    def view(g, half, part, yy, zz):
        lo, hi = bounds[part]
        rows = pl.ds(pl.multiple_of((yy * 8 + zz) * SLOT, SLOT), SLOT)
        return arrays[g][1].at[half, rows, lo:hi]

    def slot(yy, zz):
        return yy * 8 + zz

    def send(g, part, yy, zz, device, src=None):
        v = view(g, core, part, yy, zz)
        push(v if src is None else src, v, ring_s.at[g], ring_r.at[g, part, slot(yy, zz)], device)

    def forward_partner(g, part, yy, zz, src=None):
        v = view(g, core, part, yy, zz)
        push(v if src is None else src, v, part_s.at[g], part_r.at[g], partner)

    def arrived(g, part, yy, zz):
        v = view(g, core, part, yy, zz)
        pltpu.make_async_copy(v, v, ring_r.at[g, part, slot(yy, zz)]).wait()

    own_copies = []
    znext, zprev = at(y, zmove(1)), at(y, zmove(-1))
    ynext, yprev = at(ymove(1), z), at(ymove(-1), z)

    def begin(g):
        pairs[g].wait()
        merged[g] = paired[g] + arrays[g][0][core]
        c = pltpu.make_async_copy(
            merged.at[g], arrays[g][1].at[core, pl.ds(pl.multiple_of((y * 8 + z) * SLOT, SLOT), SLOT), :], own_s.at[g])
        c.start()
        own_copies.append(c)
        a, b = merged.at[g, :, 0:A_LANES], merged.at[g, :, A_LANES:HALF]
        va = view(g, core, 0, y, z)
        for d in (1, 2, 3):
            push(a, va, ring_s.at[g], ring_r.at[g, 0, slot(y, z)], at(ymove(d), z))
        send(g, 1, y, z, znext, b)
        send(g, 1, y, z, zprev, b)
        send(g, 0, y, z, znext, a)
        send(g, 0, y, z, zprev, a)
        send(g, 1, y, z, ynext, b)
        send(g, 1, y, z, yprev, b)
        forward_partner(g, 0, y, z, a)
        forward_partner(g, 1, y, z, b)

    def column(g, d):
        yy = ymove(d)
        arrived(g, 0, yy, z)
        send(g, 0, yy, z, znext)
        send(g, 0, yy, z, zprev)
        forward_partner(g, 0, yy, z)

    def b_ring(g, s, way):
        zz = zmove(-s) if way > 0 else zmove(s)
        arrived(g, 1, y, zz)
        if way > 0 and s < 4:
            send(g, 1, y, zz, znext)
        if way < 0 and s < 3:
            send(g, 1, y, zz, zprev)
        send(g, 1, y, zz, ynext)
        send(g, 1, y, zz, yprev)
        forward_partner(g, 1, y, zz)

    def a_ring(g, s, way, d):
        zz = zmove(-s) if way > 0 else zmove(s)
        yy = ymove(d)
        arrived(g, 0, yy, zz)
        if way > 0 and s < 4:
            send(g, 0, yy, zz, znext)
        if way < 0 and s < 3:
            send(g, 0, yy, zz, zprev)
        forward_partner(g, 0, yy, zz)

    def y_pass(g, zz):
        arrived(g, 1, ymove(-1), zz)
        send(g, 1, ymove(-1), zz, ynext)
        forward_partner(g, 1, ymove(-1), zz)
        arrived(g, 1, ymove(1), zz)
        forward_partner(g, 1, ymove(1), zz)

    def y_last(g, zz):
        arrived(g, 1, ymove(2), zz)
        forward_partner(g, 1, ymove(2), zz)

    def ring_steps(g):
        steps = []

        def b_hop(k):
            steps.append(functools.partial(b_ring, g, k, 1))
            if k < 4:
                steps.append(functools.partial(b_ring, g, k, -1))

        def a_hop(k):
            for d in range(4):
                steps.append(functools.partial(a_ring, g, k, 1, d))
                if k < 4:
                    steps.append(functools.partial(a_ring, g, k, -1, d))

        def y_hop(k):
            steps.append(functools.partial(y_pass, g, zmove(-k)))
            if 0 < k < 4:
                steps.append(functools.partial(y_pass, g, zmove(k)))

        def y_end(*ks):
            steps.extend(functools.partial(y_last, g, zmove(k)) for k in ks)

        b_hop(1)
        steps.extend(functools.partial(column, g, d) for d in (1, 3, 2))
        y_hop(0)
        b_hop(2)
        y_hop(1)
        a_hop(1)
        b_hop(3)
        y_hop(2)
        b_hop(4)
        y_end(0)
        a_hop(2)
        y_hop(3)
        y_end(-1, 1)
        y_hop(4)
        y_end(-2, 2)
        a_hop(3)
        y_end(-3, 3, 4)
        a_hop(4)
        return steps

    def from_partner(g):
        settle(arrays[g][1].at[1 - core], part_r.at[g])

    def settle(ref, sem):
        pltpu.make_async_copy(ref, ref, sem).wait()

    begin(0)
    weights(layer, ket, bra)
    steps = ring_steps(0)
    for step in steps[:-8]:
        step()
    for c in xcopies + own_x:
        c.wait()
    acc = jnp.zeros((ROWS, 512), jnp.float32)
    for n in range(4):
        acc += jnp.dot(left_all[n], corner_all[n], preferred_element_type=jnp.float32)
    half[...] = acc.astype(jnp.bfloat16)
    begin(1)
    for step in steps[-8:]:
        step()
    own_copies[0].wait()
    from_partner(0)

    work = compute_steps(half, right_all, ket, bra, strip, layered)
    steps = ring_steps(1)
    done = 0
    for k, compute in enumerate(work):
        compute()
        upto = int(len(steps) * ((k + 1) / len(work)) ** 1.5)
        for step in steps[done:upto]:
            step()
        done = upto
    own_copies[1].wait()
    from_partner(1)

    def start(src, dst, ss, rs, device):
        c = pltpu.make_async_remote_copy(src_ref=src, dst_ref=dst, send_sem=ss, recv_sem=rs,
                                         device_id=device, device_id_type=MESH)
        c.start()
        return c

    c1 = [None] * 3
    for pair in ((1, 0), (2, None)):
        names = [x if d is None else xs[d] for d in pair]
        project(strip, warm_all, total, part, names)
        for d in pair:
            if d is not None:
                c1[d] = start(part.at[xs[d]], got.at[d], n_s.at[d], n_r.at[d], (me, xs[d]))
    acc = part[x].astype(jnp.float32)
    for d in range(3):
        c1[d].wait_recv()
        acc += got[d].astype(jnp.float32)
    proj[x] = acc.astype(jnp.bfloat16)
    c2 = [start(proj.at[x], proj.at[x], p_s.at[d], p_r.at[d], (me, xs[d])) for d in range(3)]
    own = acc.astype(jnp.bfloat16)
    tn = (((0,), (0,)), ((), ()))
    scale = 1.0 / (448 * 49)

    def product(n):
        full = lax.dot_general(proj[n], own, tn, preferred_element_type=jnp.float32) * scale
        slab[pl.ds(pl.multiple_of(n * 112, 112), 112), :] = full[0:112]

    product(x)
    for d in (0, 2, 1):
        c2[d].wait_recv()
        product(lax.rem(x + 3 - d, 4))

    def rows(k, size):
        return pl.ds(pl.multiple_of(k * size, size), size)

    mine = y * 2 + core
    c3 = [start(slab.at[rows(yy * 2 + cc, 56)], got1.at[k], a_s.at[k], a_r.at[k], (wide_of(yy, z, cc), x))
          for k, (yy, cc) in enumerate(others)]
    acc = slab[rows(mine, 56), :]
    for k in range(7):
        c3[k].wait_recv()
        acc += got1[k]
    piece[0:56, :] = acc
    piece[56:64, :] = jnp.zeros((8, 128), jnp.float32)
    c4 = [start(piece.at[rows(zz, 8)], got2.at[k], b_s.at[k], b_r.at[k], (wide_of(y, zz, core), x))
          for k, zz in enumerate(zs)]
    acc = piece[rows(z, 8), :]
    for k in range(7):
        c4[k].wait_recv()
        acc += got2[k]
    spot = gram.at[x, y, core, rows(z, 8)]
    gram[x, y, core, rows(z, 8), :] = acc
    c5 = [start(spot, spot, c_s.at[k], c_r.at[k], at(y, zz)) for k, zz in enumerate(zs)]
    for c in c5:
        c.wait_recv()
    spot = gram.at[x, y, core, 0:56]
    c6 = [start(spot, spot, d_s.at[k], d_r.at[k], (wide_of(yy, z, core), xx)) for k, (xx, yy) in enumerate(plane)]
    start(spot, spot, f_s, f_r, partner)
    for k in (7, 8, 9, 10, 2, 1, 11, 12, 13, 14, 3, 4, 5, 6, 0):
        xx, yy = plane[k]
        c6[k].wait_recv()
        spot = gram.at[lax.rem(2 * x + 4 - xx, 4), lax.rem(2 * y + 4 - yy, 4), core, 0:56]
        start(spot, spot, f_s, f_r, partner)
    settle(gram.at[:, :, core, 0:56], f_s)
    settle(gram.at[:, :, 1 - core, 0:56], f_r)
    for c in c1 + c2 + c3 + c4 + c5 + c6:
        c.wait_send()
    for g in (0, 1):
        settle(arrays[g][1].at[core], part_s.at[g])
        settle(arrays[g][1].at[core, 0:496], ring_s.at[g])


def iota(shape, axis):
    return lax.broadcasted_iota(jnp.int32, shape, axis)


def flags(mask):
    return jnp.where(mask, 1.0, 0.0).astype(jnp.bfloat16)


def mm(a, b):
    return jnp.dot(a, b, preferred_element_type=jnp.float32).astype(jnp.bfloat16)


def mm_nt(a, b):
    return lax.dot_general(a, b, (((1,), (1,)), ((), ())), preferred_element_type=jnp.float32).astype(jnp.bfloat16)


def weights(layer, ket, bra):
    row, col = iota((784, 49), 0), iota((784, 49), 1)
    low = row & 15
    spread = mm_nt(flags((row >> 4 == col) & (low < 7)), layer[0])
    spread += mm_nt(flags((row >> 4 == col) & (low >= 7) & (low < 14)), layer[1])
    row, col = iota((49, ROWS), 0), iota((49, ROWS), 1)
    q, u = col >> 3, col & 7
    full = mm(spread, flags((u < 7) & (q < 49) & (row == u * 7 + ((q * 37) >> 8))))
    row, col = iota((784, ROWS), 0), iota((784, ROWS), 1)
    low, q = row & 15, col >> 3
    same = jnp.where(low < 7, low, low - 7) == q - 7 * ((q * 37) >> 8)
    ket[...] = jnp.where(same, full.astype(jnp.float32), 0.0).astype(jnp.bfloat16)
    row, col = iota((56, 49), 0), iota((56, 49), 1)
    lead = flags((row & 7 < 7) & (col == (row & 7) * 7 + (row >> 3)))
    row, col = iota((49, 112), 0), iota((49, 112), 1)
    low = col & 15
    acc = jnp.zeros((56, 112), jnp.float32)
    for s in range(2):
        ok = (low >= 7 * s) & (low < 7 * s + 7) & (row == (col >> 4) * 7 + low - 7 * s)
        acc += mm(mm_nt(lead, layer[s]), flags(ok)).astype(jnp.float32)
    bra[...] = acc.astype(jnp.bfloat16)


def compute_steps(half, right, ket, bra, strip, layered):
    def strips(h, chunk):
        res = jnp.dot(half[...], right[h, :, chunk * 640:(chunk + 1) * 640], preferred_element_type=jnp.float32)
        for j in range(5):
            first = (h * 25 + chunk * 5 + j) * 8
            strip[:, first:first + 8, :] = res[:, j * 128:(j + 1) * 128].reshape(50, 8, 128)

    def kets(first):
        @pl.loop(first, first + 5)
        def _(t):
            x = jnp.concatenate([strip[2 * t].astype(jnp.bfloat16), strip[2 * t + 1].astype(jnp.bfloat16)], axis=1)
            res = jnp.dot(ket[...], x, preferred_element_type=jnp.float32).astype(jnp.bfloat16)
            for j in range(2):
                rows = pl.ds(pl.multiple_of((2 * t + j) * 16, 16), 16)
                layered[:, rows, :] = res[:, j * 128:(j + 1) * 128].reshape(49, 16, 128)

    def clear():
        strip[49] = jnp.zeros((ROWS, 128), jnp.float32)
        strip[:, 392:400, :] = jnp.zeros((50, 8, 128), jnp.float32)

    def bras(d):
        @pl.loop(0, 7)
        def _(r):
            x = jnp.concatenate([layered[d * 7 + r, i * 112:(i + 1) * 112, :] for i in range(7)], axis=1)
            res = jnp.dot(bra[...], x, preferred_element_type=jnp.float32)
            for i in range(7):
                for s in range(7):
                    strip[r * 7 + s, (i * 7 + d) * 8:(i * 7 + d) * 8 + 8, :] = (
                        res[s * 8:(s + 1) * 8, i * 128:(i + 1) * 128])

    work = [functools.partial(strips, h, chunk) for h in range(2) for chunk in range(5)]
    work += [functools.partial(kets, 5 * t) for t in range(5)]
    work += [clear]
    work += [functools.partial(bras, d) for d in range(7)]
    return work


def project(enlarged, warm, total, part, names):
    total[...] = jnp.zeros_like(total)
    spans = [pl.ds(pl.multiple_of(n * 128, 128), 128) for n in names]
    for h in range(2):
        @pl.loop(0, 5)
        def _(chunk):
            cols = pl.ds(pl.multiple_of(chunk * 640, 640), 640)
            x = jnp.concatenate(
                [enlarged[h * 25 + chunk * 5 + j].astype(jnp.bfloat16) for j in range(5)], axis=1)
            w = jnp.concatenate([warm[h, span, cols] for span in spans], axis=0)
            total[...] += lax.dot_general(x, w, (((1,), (1,)), ((), ())), preferred_element_type=jnp.float32)
    row, col = iota((128, 128), 0), iota((128, 128), 1)
    pick = flags((row & 15 < 14) & (col == (row >> 4) * 14 + (row & 15)))
    for k, n in enumerate(names):
        part[n] = mm(total[:, k * 128:(k + 1) * 128].astype(jnp.bfloat16), pick)


def gathers(right, warm, left, corner, layer):
    dma = pltpu.SemaphoreType.DMA
    vm = pl.BlockSpec(memory_space=pltpu.VMEM)
    return pl.pallas_call(
        gather_kernel,
        out_shape=[
            jax.ShapeDtypeStruct((4, ROWS, 128), jnp.bfloat16),
            jax.ShapeDtypeStruct((4, 4, 2, 64, 128), jnp.float32),
        ],
        in_specs=[vm] * 5,
        out_specs=[vm, vm],
        scratch_shapes=[
            pltpu.VMEM((2, 32 * SLOT, HALF), jnp.bfloat16),
            pltpu.VMEM((2, 32 * SLOT, HALF), jnp.bfloat16),
            pltpu.VMEM((4, ROWS, 128), jnp.bfloat16),
            pltpu.VMEM((4, 128, 512), jnp.bfloat16),
            pltpu.VMEM((ROWS, 512), jnp.bfloat16),
            pltpu.VMEM((50, ROWS, 128), jnp.float32),
            pltpu.VMEM((49, 800, 128), jnp.bfloat16),
            pltpu.VMEM((ROWS, 256), jnp.float32),
            pltpu.VMEM((784, ROWS), jnp.bfloat16),
            pltpu.VMEM((56, 112), jnp.bfloat16),
            pltpu.VMEM((2, SLOT, HALF), jnp.bfloat16),
            pltpu.VMEM((2, SLOT, HALF), jnp.bfloat16),
            pltpu.VMEM((4, ROWS, 128), jnp.bfloat16),
            pltpu.VMEM((3, ROWS, 128), jnp.bfloat16),
            pltpu.VMEM((448, 128), jnp.float32),
            pltpu.VMEM((7, 56, 128), jnp.float32),
            pltpu.VMEM((64, 128), jnp.float32),
            pltpu.VMEM((7, 8, 128), jnp.float32),
            dma((2,)), dma((2,)), dma((4,)), dma((2, 2, 32)), dma((2,)), dma((2,)), dma((2,)), dma((2, 3)), dma((2, 3)),
            dma((3,)), dma((3,)), dma((3,)), dma((3,)), dma((7,)), dma((7,)), dma((7,)), dma((7,)),
            dma((7,)), dma((7,)), dma((15,)), dma((15,)), dma, dma,
        ],
        compiler_params=pltpu.CompilerParams(collective_id=1, has_side_effects=True, vmem_limit_bytes=46 * MIB),
        name="gathers",
    )(right, warm, left, corner, layer)


def eliminate(diag):
    n = BLOCK
    row_id, col_id = iota((n, n), 0), iota((n, n), 1)
    wide = jnp.concatenate([diag, jnp.where(row_id == col_id, 1.0, 0.0).astype(jnp.float32)], axis=1)
    groups = [wide[8 * g:8 * g + 8] for g in range(n // 8)]
    sub = iota((8, 2 * n), 0)

    def full(v):
        return jnp.broadcast_to(v, (8, 2 * n))

    for g in range(n // 8):
        k, own = 8 * g, groups[g]
        rows = [full(own[i:i + 1, :]) for i in range(8)]
        cols = [full(own[:, k + j:k + j + 1]) for j in range(8)]
        e = {(i, j): full(cols[j][i:i + 1, :]) for i in range(8) for j in range(i, 8)}
        scaled, s = [], {}
        for r in range(8):
            inv = 1.0 / e[r, r]
            scaled.append(rows[r] * inv)
            for j in range(r + 1, 8):
                s[r, j] = e[r, j] * inv
            for i in range(r + 1, 8):
                rows[i] = rows[i] - e[r, i] * scaled[r]
                for j in range(i, 8):
                    e[i, j] = e[i, j] - e[r, i] * s[r, j]
        for h in range(g + 1, n // 8):
            below = groups[h]
            c = [full(below[:, k + j:k + j + 1]) for j in range(8)]
            for r in range(8):
                below = below - c[r] * scaled[r]
                for j in range(r + 1, 8):
                    c[j] = c[j] - c[r] * s[r, j]
            groups[h] = below
        for i in range(1, 8):
            own = jnp.where(sub == i, rows[i], own)
        groups[g] = own
    wide = jnp.concatenate(groups, axis=0)
    upper, lower = wide[:, :n], wide[:, n:]
    d = jnp.sum(jnp.where(row_id == col_id, upper, 0.0), axis=1, keepdims=True)
    root = lax.rsqrt(d)
    root = root * (1.5 - 0.5 * d * root * root)
    return jnp.where(row_id <= col_id, upper * root, 0.0), jnp.where(row_id >= col_id, lower * root, 0.0)


def factor_kernel(gram, proj, r_ref, out, work):
    n = 448
    x = lax.axis_index("narrow")
    for a in range(4):
        for b in range(4):
            for c in range(2):
                first = a * 112 + c * 56
                work[first:first + 56, b * 112:(b + 1) * 112] = gram[b, a, c, 0:56, 0:112]
    r_ref[...] = jnp.zeros_like(r_ref)
    col = lax.broadcasted_iota(jnp.int32, (BLOCK, n), 1)
    row = lax.broadcasted_iota(jnp.int32, (BLOCK, n), 0)
    ahead = work[0:BLOCK, 0:BLOCK]
    for b in range(n // BLOCK):
        lo, hi = b * BLOCK, (b + 1) * BLOCK
        r, inverse = eliminate(ahead)
        if hi < n:
            near = jnp.dot(inverse, work[lo:hi, hi:hi + BLOCK], precision=HI, preferred_element_type=jnp.float32)
            ahead = work[hi:hi + BLOCK, hi:hi + BLOCK] - lax.dot_general(
                near, near, (((0,), (0,)), ((), ())), precision=HI, preferred_element_type=jnp.float32)
        inside = (col >= lo) & (col < hi)
        src = jnp.where(inside, jnp.where(col - lo == row, 1.0, 0.0), work[lo:hi, :])
        full = jnp.dot(inverse, src, precision=HI, preferred_element_type=jnp.float32)
        work[lo:hi, :] = jnp.where(col < hi, full, 0.0)
        rest = jnp.where(col >= hi, full, 0.0)
        r_ref[lo:hi, :] = rest
        r_ref[lo:hi, lo:hi] = r
        if hi < n:
            at = lax.broadcasted_iota(jnp.int32, (n - hi, n), 1)
            old = jnp.where((at >= lo) & (at < hi), 0.0, work[hi:, :])
            work[hi:, :] = old - lax.dot_general(rest[:, hi:], full, (((0,), (0,)), ((), ())), precision=HI,
                                                 preferred_element_type=jnp.float32)
    own = work[pl.ds(pl.multiple_of(x * 112, 8), 112), :]
    nt = (((1,), (1,)), ((), ()))
    acc = jnp.zeros((ROWS, 112), jnp.float32)
    for b in range(4):
        acc += lax.dot_general(proj[b][:, 0:112].astype(jnp.float32), own[:, b * 112:(b + 1) * 112], nt, precision=HI,
                               preferred_element_type=jnp.float32)
    out[...] = acc


def factor(gram, proj):
    vm = pl.BlockSpec(memory_space=pltpu.VMEM)
    return pl.pallas_call(
        factor_kernel,
        out_shape=[jax.ShapeDtypeStruct((448, 448), jnp.float32), jax.ShapeDtypeStruct((ROWS, 112), jnp.float32)],
        in_specs=[vm, vm],
        out_specs=[vm, vm],
        scratch_shapes=[pltpu.VMEM((448, 448), jnp.float32)],
        compiler_params=pltpu.CompilerParams(vmem_limit_bytes=40 * MIB),
        name="factor",
    )(gram, proj)


def shard_rows(block, core):
    rows = jnp.pad(block, ((0, 0), (0, 1), (0, 16))).reshape(7, 2, HALF).transpose(1, 0, 2)
    return jnp.where(core == 0, jnp.pad(rows, ((0, 0), (0, 9), (0, 0))), jnp.pad(rows, ((0, 0), (7, 2), (0, 0))))


def on_device(left_edge, corner, right_edge, single_layer, warm_basis):
    core = lax.axis_index("wide") % 2
    right = shard_rows(right_edge, core)
    warm = shard_rows(warm_basis.transpose(2, 0, 1), core)
    left = left_edge.reshape(7, 7, 7, 112).transpose(0, 2, 1, 3)
    left = jnp.pad(left, ((0, 0), (0, 0), (0, 1), (0, 16))).reshape(392, 128)
    left = jnp.pad(left, ((0, 8), (0, 0)))
    corner = jnp.pad(corner.reshape(112, 32, 14), ((0, 16), (0, 0), (0, 2))).reshape(128, 512)
    proj, gram = gathers(right, warm, left, corner, single_layer.reshape(2, 49, 49))
    r_factor, rows = factor(gram, proj)
    new_basis = rows[:392].reshape(7, 7, 8, 112)[:, :, :7].reshape(7, 49, 112)
    return new_basis, r_factor


def solution(mesh):
    placed = (
        P("wide", None, "narrow"),
        P("narrow", None),
        P("wide", None, "narrow"),
        P(),
        P(None, "narrow", "wide"),
    )
    return jax.shard_map(
        on_device,
        mesh=mesh,
        in_specs=placed,
        out_specs=(P("wide", None, "narrow"), P()),
        check_vma=False,
    )
```

```python
import functools

import jax
import jax.numpy as jnp
from jax import lax
from jax.experimental import pallas as pl
from jax.experimental.pallas import tpu as pltpu
from jax.sharding import PartitionSpec as P

BOND = 7
BLOCK = 64
SLOT = 16
HALF = 3200
A_LANES = 1280
ROWS = 400
HI = lax.Precision.HIGHEST
MESH = pl.DeviceIdType.MESH
MIB = 1 << 20


def place():
    wide = lax.axis_index("wide")
    core = lax.rem(wide, 2)
    z = lax.rem(lax.div(wide, 2), 8)
    y = lax.div(wide, 16)
    return y, z, core, lax.axis_index("narrow")


def wide_of(y, z, core):
    return (y * 8 + z) * 2 + core


def greet(peers):
    barrier = pltpu.get_barrier_semaphore()
    for peer in peers:
        pl.semaphore_signal(barrier, inc=1, device_id=peer, device_id_type=MESH)
    pl.semaphore_wait(barrier, len(peers))


def gather_kernel(right, warm, left, corner, layer, proj, gram,
                  right_all, warm_all, left_all, corner_all, half, strip, layered, total, ket, bra,
                  paired, merged, part, got, slab, got1, piece, got2,
                  pair_s, pair_r, own_s, ring_r, ring_s, part_s, part_r, x_s, x_r,
                  n_s, n_r, p_s, p_r, a_s, a_r, b_s, b_r, c_s, c_r, d_s, d_r, f_s, f_r):
    y, z, core, x = place()
    zdir = 1 - 2 * core

    def zmove(k):
        return lax.rem(z + 8 + k * zdir, 8)

    def ymove(k):
        return lax.rem(y + 4 + k * zdir, 4)

    def at(yy, zz, cc=None):
        return (wide_of(yy, zz, core if cc is None else cc), x)

    partner = at(y, z, 1 - core)
    others = [(lax.rem(y + k // 2, 4), lax.rem(core + k % 2, 2)) for k in range(1, 8)]
    xs = [lax.rem(x + d, 4) for d in (1, 2, 3)]
    zs = [lax.rem(z + d, 8) for d in range(1, 8)]
    me = wide_of(y, z, core)
    plane = [(lax.rem(x + k // 4, 4), lax.rem(y + k % 4, 4)) for k in (10, 2, 8, 6, 14, 9, 11, 1, 3, 4, 12, 5, 7, 13, 15)]
    greet([at(yy, z, cc) for yy, cc in others] + [at(y, zz) for zz in zs]
          + [(wide_of(lax.rem(y + k % 4, 4), z, core), lax.rem(x + k // 4, 4)) for k in range(4, 16)])

    def push(src, dst, ss, rs, device):
        c = pltpu.make_async_remote_copy(src_ref=src, dst_ref=dst, send_sem=ss, recv_sem=rs,
                                         device_id=device, device_id_type=MESH)
        c.start()

    arrays = ((right, right_all), (warm, warm_all))
    pairs = []
    for g, (src, _) in enumerate(arrays):
        c = pltpu.make_async_remote_copy(src_ref=src.at[1 - core], dst_ref=paired.at[g], send_sem=pair_s.at[g],
                                         recv_sem=pair_r.at[g], device_id=partner, device_id_type=MESH)
        c.start()
        pairs.append(c)
    xcopies = []
    for src, dst, k in ((left, left_all, 0), (corner, corner_all, 1)):
        for d in (1, 2, 3):
            c = pltpu.make_async_remote_copy(
                src_ref=src, dst_ref=dst.at[x], send_sem=x_s.at[k, d - 1], recv_sem=x_r.at[k, d - 1],
                device_id=(wide_of(y, z, core), lax.rem(x + d, 4)), device_id_type=MESH)
            c.start()
            xcopies.append(c)
    own_x = []
    for src, dst, k in ((left, left_all, 0), (corner, corner_all, 1)):
        c = pltpu.make_async_copy(src, dst.at[x], own_s.at[2 + k])
        c.start()
        own_x.append(c)

    bounds = ((0, A_LANES), (A_LANES, HALF))

    def view(g, half, part, yy, zz):
        lo, hi = bounds[part]
        rows = pl.ds(pl.multiple_of((yy * 8 + zz) * SLOT, SLOT), SLOT)
        return arrays[g][1].at[half, rows, lo:hi]

    def slot(yy, zz):
        return yy * 8 + zz

    def send(g, part, yy, zz, device, src=None):
        v = view(g, core, part, yy, zz)
        push(v if src is None else src, v, ring_s.at[g], ring_r.at[g, part, slot(yy, zz)], device)

    def forward_partner(g, part, yy, zz, src=None):
        v = view(g, core, part, yy, zz)
        push(v if src is None else src, v, part_s.at[g], part_r.at[g], partner)

    def arrived(g, part, yy, zz):
        v = view(g, core, part, yy, zz)
        pltpu.make_async_copy(v, v, ring_r.at[g, part, slot(yy, zz)]).wait()

    own_copies = []
    znext, zprev = at(y, zmove(1)), at(y, zmove(-1))
    ynext, yprev = at(ymove(1), z), at(ymove(-1), z)

    def begin(g):
        pairs[g].wait()
        merged[g] = paired[g] + arrays[g][0][core]
        c = pltpu.make_async_copy(
            merged.at[g], arrays[g][1].at[core, pl.ds(pl.multiple_of((y * 8 + z) * SLOT, SLOT), SLOT), :], own_s.at[g])
        c.start()
        own_copies.append(c)
        a, b = merged.at[g, :, 0:A_LANES], merged.at[g, :, A_LANES:HALF]
        va = view(g, core, 0, y, z)
        for d in (1, 2, 3):
            push(a, va, ring_s.at[g], ring_r.at[g, 0, slot(y, z)], at(ymove(d), z))
        send(g, 1, y, z, znext, b)
        send(g, 1, y, z, zprev, b)
        send(g, 0, y, z, znext, a)
        send(g, 0, y, z, zprev, a)
        send(g, 1, y, z, ynext, b)
        send(g, 1, y, z, yprev, b)
        forward_partner(g, 0, y, z, a)
        forward_partner(g, 1, y, z, b)

    def column(g, d):
        yy = ymove(d)
        arrived(g, 0, yy, z)
        send(g, 0, yy, z, znext)
        send(g, 0, yy, z, zprev)
        forward_partner(g, 0, yy, z)

    def b_ring(g, s, way):
        zz = zmove(-s) if way > 0 else zmove(s)
        arrived(g, 1, y, zz)
        if way > 0 and s < 4:
            send(g, 1, y, zz, znext)
        if way < 0 and s < 3:
            send(g, 1, y, zz, zprev)
        send(g, 1, y, zz, ynext)
        send(g, 1, y, zz, yprev)
        forward_partner(g, 1, y, zz)

    def a_ring(g, s, way, d):
        zz = zmove(-s) if way > 0 else zmove(s)
        yy = ymove(d)
        arrived(g, 0, yy, zz)
        if way > 0 and s < 4:
            send(g, 0, yy, zz, znext)
        if way < 0 and s < 3:
            send(g, 0, yy, zz, zprev)
        forward_partner(g, 0, yy, zz)

    def y_pass(g, zz):
        arrived(g, 1, ymove(-1), zz)
        send(g, 1, ymove(-1), zz, ynext)
        forward_partner(g, 1, ymove(-1), zz)
        arrived(g, 1, ymove(1), zz)
        forward_partner(g, 1, ymove(1), zz)

    def y_last(g, zz):
        arrived(g, 1, ymove(2), zz)
        forward_partner(g, 1, ymove(2), zz)

    def ring_steps(g):
        steps = []

        def b_hop(k):
            steps.append(functools.partial(b_ring, g, k, 1))
            if k < 4:
                steps.append(functools.partial(b_ring, g, k, -1))

        def a_hop(k):
            for d in range(4):
                steps.append(functools.partial(a_ring, g, k, 1, d))
                if k < 4:
                    steps.append(functools.partial(a_ring, g, k, -1, d))

        def y_hop(k):
            steps.append(functools.partial(y_pass, g, zmove(-k)))
            if 0 < k < 4:
                steps.append(functools.partial(y_pass, g, zmove(k)))

        def y_end(*ks):
            steps.extend(functools.partial(y_last, g, zmove(k)) for k in ks)

        b_hop(1)
        steps.extend(functools.partial(column, g, d) for d in (1, 3, 2))
        y_hop(0)
        b_hop(2)
        y_hop(1)
        a_hop(1)
        b_hop(3)
        y_hop(2)
        b_hop(4)
        y_end(0)
        a_hop(2)
        y_hop(3)
        y_end(-1, 1)
        y_hop(4)
        y_end(-2, 2)
        a_hop(3)
        y_end(-3, 3, 4)
        a_hop(4)
        return steps

    def from_partner(g):
        settle(arrays[g][1].at[1 - core], part_r.at[g])

    def settle(ref, sem):
        pltpu.make_async_copy(ref, ref, sem).wait()

    begin(0)
    weights(layer, ket, bra)
    steps = ring_steps(0)
    for step in steps[:-8]:
        step()
    for c in xcopies + own_x:
        c.wait()
    acc = jnp.zeros((ROWS, 512), jnp.float32)
    for n in range(4):
        acc += jnp.dot(left_all[n], corner_all[n], preferred_element_type=jnp.float32)
    half[...] = acc.astype(jnp.bfloat16)
    begin(1)
    for step in steps[-8:]:
        step()
    own_copies[0].wait()
    from_partner(0)

    work = compute_steps(half, right_all, ket, bra, strip, layered)
    steps = ring_steps(1)
    done = 0
    for k, compute in enumerate(work):
        compute()
        upto = int(len(steps) * ((k + 1) / len(work)) ** 1.5)
        for step in steps[done:upto]:
            step()
        done = upto
    own_copies[1].wait()
    from_partner(1)

    def start(src, dst, ss, rs, device):
        c = pltpu.make_async_remote_copy(src_ref=src, dst_ref=dst, send_sem=ss, recv_sem=rs,
                                         device_id=device, device_id_type=MESH)
        c.start()
        return c

    c1 = [None] * 3
    for pair in ((1, 0), (2, None)):
        names = [x if d is None else xs[d] for d in pair]
        project(strip, warm_all, total, part, names)
        for d in pair:
            if d is not None:
                c1[d] = start(part.at[xs[d]], got.at[d], n_s.at[d], n_r.at[d], (me, xs[d]))
    acc = part[x].astype(jnp.float32)
    for d in range(3):
        c1[d].wait_recv()
        acc += got[d].astype(jnp.float32)
    proj[x] = acc.astype(jnp.bfloat16)
    c2 = [start(proj.at[x], proj.at[x], p_s.at[d], p_r.at[d], (me, xs[d])) for d in range(3)]
    own = acc.astype(jnp.bfloat16)
    tn = (((0,), (0,)), ((), ()))
    scale = 1.0 / (448 * 49)

    def product(n):
        full = lax.dot_general(proj[n], own, tn, preferred_element_type=jnp.float32) * scale
        slab[pl.ds(pl.multiple_of(n * 112, 112), 112), :] = full[0:112]

    product(x)
    for d in (0, 2, 1):
        c2[d].wait_recv()
        product(lax.rem(x + 3 - d, 4))

    def rows(k, size):
        return pl.ds(pl.multiple_of(k * size, size), size)

    mine = y * 2 + core
    c3 = [start(slab.at[rows(yy * 2 + cc, 56)], got1.at[k], a_s.at[k], a_r.at[k], (wide_of(yy, z, cc), x))
          for k, (yy, cc) in enumerate(others)]
    acc = slab[rows(mine, 56), :]
    for k in range(7):
        c3[k].wait_recv()
        acc += got1[k]
    piece[0:56, :] = acc
    piece[56:64, :] = jnp.zeros((8, 128), jnp.float32)
    c4 = [start(piece.at[rows(zz, 8)], got2.at[k], b_s.at[k], b_r.at[k], (wide_of(y, zz, core), x))
          for k, zz in enumerate(zs)]
    acc = piece[rows(z, 8), :]
    for k in range(7):
        c4[k].wait_recv()
        acc += got2[k]
    spot = gram.at[x, y, core, rows(z, 8)]
    gram[x, y, core, rows(z, 8), :] = acc
    c5 = [start(spot, spot, c_s.at[k], c_r.at[k], at(y, zz)) for k, zz in enumerate(zs)]
    for c in c5:
        c.wait_recv()
    spot = gram.at[x, y, core, 0:56]
    c6 = [start(spot, spot, d_s.at[k], d_r.at[k], (wide_of(yy, z, core), xx)) for k, (xx, yy) in enumerate(plane)]
    start(spot, spot, f_s, f_r, partner)
    for k in (7, 8, 9, 10, 2, 1, 11, 12, 13, 14, 3, 4, 5, 6, 0):
        xx, yy = plane[k]
        c6[k].wait_recv()
        spot = gram.at[lax.rem(2 * x + 4 - xx, 4), lax.rem(2 * y + 4 - yy, 4), core, 0:56]
        start(spot, spot, f_s, f_r, partner)
    settle(gram.at[:, :, core, 0:56], f_s)
    settle(gram.at[:, :, 1 - core, 0:56], f_r)
    for c in c1 + c2 + c3 + c4 + c5 + c6:
        c.wait_send()
    for g in (0, 1):
        settle(arrays[g][1].at[core], part_s.at[g])
        settle(arrays[g][1].at[core, 0:496], ring_s.at[g])


def iota(shape, axis):
    return lax.broadcasted_iota(jnp.int32, shape, axis)


def flags(mask):
    return jnp.where(mask, 1.0, 0.0).astype(jnp.bfloat16)


def mm(a, b):
    return jnp.dot(a, b, preferred_element_type=jnp.float32).astype(jnp.bfloat16)


def mm_nt(a, b):
    return lax.dot_general(a, b, (((1,), (1,)), ((), ())), preferred_element_type=jnp.float32).astype(jnp.bfloat16)


def weights(layer, ket, bra):
    row, col = iota((784, 49), 0), iota((784, 49), 1)
    low = row & 15
    spread = mm_nt(flags((row >> 4 == col) & (low < 7)), layer[0])
    spread += mm_nt(flags((row >> 4 == col) & (low >= 7) & (low < 14)), layer[1])
    row, col = iota((49, ROWS), 0), iota((49, ROWS), 1)
    q, u = col >> 3, col & 7
    full = mm(spread, flags((u < 7) & (q < 49) & (row == u * 7 + ((q * 37) >> 8))))
    row, col = iota((784, ROWS), 0), iota((784, ROWS), 1)
    low, q = row & 15, col >> 3
    same = jnp.where(low < 7, low, low - 7) == q - 7 * ((q * 37) >> 8)
    ket[...] = jnp.where(same, full.astype(jnp.float32), 0.0).astype(jnp.bfloat16)
    row, col = iota((56, 49), 0), iota((56, 49), 1)
    lead = flags((row & 7 < 7) & (col == (row & 7) * 7 + (row >> 3)))
    row, col = iota((49, 112), 0), iota((49, 112), 1)
    low = col & 15
    acc = jnp.zeros((56, 112), jnp.float32)
    for s in range(2):
        ok = (low >= 7 * s) & (low < 7 * s + 7) & (row == (col >> 4) * 7 + low - 7 * s)
        acc += mm(mm_nt(lead, layer[s]), flags(ok)).astype(jnp.float32)
    bra[...] = acc.astype(jnp.bfloat16)


def compute_steps(half, right, ket, bra, strip, layered):
    def strips(h, chunk):
        res = jnp.dot(half[...], right[h, :, chunk * 640:(chunk + 1) * 640], preferred_element_type=jnp.float32)
        for j in range(5):
            first = (h * 25 + chunk * 5 + j) * 8
            strip[:, first:first + 8, :] = res[:, j * 128:(j + 1) * 128].reshape(50, 8, 128)

    def kets(first):
        @pl.loop(first, first + 5)
        def _(t):
            x = jnp.concatenate([strip[2 * t].astype(jnp.bfloat16), strip[2 * t + 1].astype(jnp.bfloat16)], axis=1)
            res = jnp.dot(ket[...], x, preferred_element_type=jnp.float32).astype(jnp.bfloat16)
            for j in range(2):
                rows = pl.ds(pl.multiple_of((2 * t + j) * 16, 16), 16)
                layered[:, rows, :] = res[:, j * 128:(j + 1) * 128].reshape(49, 16, 128)

    def clear():
        strip[49] = jnp.zeros((ROWS, 128), jnp.float32)
        strip[:, 392:400, :] = jnp.zeros((50, 8, 128), jnp.float32)

    def bras(d):
        @pl.loop(0, 7)
        def _(r):
            x = jnp.concatenate([layered[d * 7 + r, i * 112:(i + 1) * 112, :] for i in range(7)], axis=1)
            res = jnp.dot(bra[...], x, preferred_element_type=jnp.float32)
            for i in range(7):
                for s in range(7):
                    strip[r * 7 + s, (i * 7 + d) * 8:(i * 7 + d) * 8 + 8, :] = (
                        res[s * 8:(s + 1) * 8, i * 128:(i + 1) * 128])

    work = [functools.partial(strips, h, chunk) for h in range(2) for chunk in range(5)]
    work += [functools.partial(kets, 5 * t) for t in range(5)]
    work += [clear]
    work += [functools.partial(bras, d) for d in range(7)]
    return work


def project(enlarged, warm, total, part, names):
    total[...] = jnp.zeros_like(total)
    spans = [pl.ds(pl.multiple_of(n * 128, 128), 128) for n in names]
    for h in range(2):
        @pl.loop(0, 5)
        def _(chunk):
            cols = pl.ds(pl.multiple_of(chunk * 640, 640), 640)
            x = jnp.concatenate(
                [enlarged[h * 25 + chunk * 5 + j].astype(jnp.bfloat16) for j in range(5)], axis=1)
            w = jnp.concatenate([warm[h, span, cols] for span in spans], axis=0)
            total[...] += lax.dot_general(x, w, (((1,), (1,)), ((), ())), preferred_element_type=jnp.float32)
    row, col = iota((128, 128), 0), iota((128, 128), 1)
    pick = flags((row & 15 < 14) & (col == (row >> 4) * 14 + (row & 15)))
    for k, n in enumerate(names):
        part[n] = mm(total[:, k * 128:(k + 1) * 128].astype(jnp.bfloat16), pick)


def gathers(right, warm, left, corner, layer):
    dma = pltpu.SemaphoreType.DMA
    vm = pl.BlockSpec(memory_space=pltpu.VMEM)
    return pl.pallas_call(
        gather_kernel,
        out_shape=[
            jax.ShapeDtypeStruct((4, ROWS, 128), jnp.bfloat16),
            jax.ShapeDtypeStruct((4, 4, 2, 64, 128), jnp.float32),
        ],
        in_specs=[vm] * 5,
        out_specs=[vm, vm],
        scratch_shapes=[
            pltpu.VMEM((2, 32 * SLOT, HALF), jnp.bfloat16),
            pltpu.VMEM((2, 32 * SLOT, HALF), jnp.bfloat16),
            pltpu.VMEM((4, ROWS, 128), jnp.bfloat16),
            pltpu.VMEM((4, 128, 512), jnp.bfloat16),
            pltpu.VMEM((ROWS, 512), jnp.bfloat16),
            pltpu.VMEM((50, ROWS, 128), jnp.float32),
            pltpu.VMEM((49, 800, 128), jnp.bfloat16),
            pltpu.VMEM((ROWS, 256), jnp.float32),
            pltpu.VMEM((784, ROWS), jnp.bfloat16),
            pltpu.VMEM((56, 112), jnp.bfloat16),
            pltpu.VMEM((2, SLOT, HALF), jnp.bfloat16),
            pltpu.VMEM((2, SLOT, HALF), jnp.bfloat16),
            pltpu.VMEM((4, ROWS, 128), jnp.bfloat16),
            pltpu.VMEM((3, ROWS, 128), jnp.bfloat16),
            pltpu.VMEM((448, 128), jnp.float32),
            pltpu.VMEM((7, 56, 128), jnp.float32),
            pltpu.VMEM((64, 128), jnp.float32),
            pltpu.VMEM((7, 8, 128), jnp.float32),
            dma((2,)), dma((2,)), dma((4,)), dma((2, 2, 32)), dma((2,)), dma((2,)), dma((2,)), dma((2, 3)), dma((2, 3)),
            dma((3,)), dma((3,)), dma((3,)), dma((3,)), dma((7,)), dma((7,)), dma((7,)), dma((7,)),
            dma((7,)), dma((7,)), dma((15,)), dma((15,)), dma, dma,
        ],
        compiler_params=pltpu.CompilerParams(collective_id=1, has_side_effects=True, vmem_limit_bytes=46 * MIB),
        name="gathers",
    )(right, warm, left, corner, layer)


def eliminate(diag):
    n = BLOCK
    row_id, col_id = iota((n, n), 0), iota((n, n), 1)
    wide = jnp.concatenate([diag, jnp.where(row_id == col_id, 1.0, 0.0).astype(jnp.float32)], axis=1)
    groups = [wide[8 * g:8 * g + 8] for g in range(n // 8)]
    sub = iota((8, 2 * n), 0)

    def full(v):
        return jnp.broadcast_to(v, (8, 2 * n))

    for g in range(n // 8):
        k, own = 8 * g, groups[g]
        rows = [full(own[i:i + 1, :]) for i in range(8)]
        cols = [full(own[:, k + j:k + j + 1]) for j in range(8)]
        e = {(i, j): full(cols[j][i:i + 1, :]) for i in range(8) for j in range(i, 8)}
        scaled, s = [], {}
        for r in range(8):
            inv = 1.0 / e[r, r]
            scaled.append(rows[r] * inv)
            for j in range(r + 1, 8):
                s[r, j] = e[r, j] * inv
            for i in range(r + 1, 8):
                rows[i] = rows[i] - e[r, i] * scaled[r]
                for j in range(i, 8):
                    e[i, j] = e[i, j] - e[r, i] * s[r, j]
        for h in range(g + 1, n // 8):
            below = groups[h]
            c = [full(below[:, k + j:k + j + 1]) for j in range(8)]
            for r in range(8):
                below = below - c[r] * scaled[r]
                for j in range(r + 1, 8):
                    c[j] = c[j] - c[r] * s[r, j]
            groups[h] = below
        for i in range(1, 8):
            own = jnp.where(sub == i, rows[i], own)
        groups[g] = own
    wide = jnp.concatenate(groups, axis=0)
    upper, lower = wide[:, :n], wide[:, n:]
    d = jnp.sum(jnp.where(row_id == col_id, upper, 0.0), axis=1, keepdims=True)
    root = lax.rsqrt(d)
    root = root * (1.5 - 0.5 * d * root * root)
    return jnp.where(row_id <= col_id, upper * root, 0.0), jnp.where(row_id >= col_id, lower * root, 0.0)


def factor_kernel(gram, proj, r_ref, out, work):
    n = 448
    x = lax.axis_index("narrow")
    for a in range(4):
        for b in range(4):
            for c in range(2):
                first = a * 112 + c * 56
                work[first:first + 56, b * 112:(b + 1) * 112] = gram[b, a, c, 0:56, 0:112]
    r_ref[...] = jnp.zeros_like(r_ref)
    col = lax.broadcasted_iota(jnp.int32, (BLOCK, n), 1)
    row = lax.broadcasted_iota(jnp.int32, (BLOCK, n), 0)
    ahead = work[0:BLOCK, 0:BLOCK]
    for b in range(n // BLOCK):
        lo, hi = b * BLOCK, (b + 1) * BLOCK
        r, inverse = eliminate(ahead)
        if hi < n:
            near = jnp.dot(inverse, work[lo:hi, hi:hi + BLOCK], precision=HI, preferred_element_type=jnp.float32)
            ahead = work[hi:hi + BLOCK, hi:hi + BLOCK] - lax.dot_general(
                near, near, (((0,), (0,)), ((), ())), precision=HI, preferred_element_type=jnp.float32)
        inside = (col >= lo) & (col < hi)
        src = jnp.where(inside, jnp.where(col - lo == row, 1.0, 0.0), work[lo:hi, :])
        full = jnp.dot(inverse, src, precision=HI, preferred_element_type=jnp.float32)
        work[lo:hi, :] = jnp.where(col < hi, full, 0.0)
        rest = jnp.where(col >= hi, full, 0.0)
        r_ref[lo:hi, :] = rest
        r_ref[lo:hi, lo:hi] = r
        if hi < n:
            at = lax.broadcasted_iota(jnp.int32, (n - hi, n), 1)
            old = jnp.where((at >= lo) & (at < hi), 0.0, work[hi:, :])
            work[hi:, :] = old - lax.dot_general(rest[:, hi:], full, (((0,), (0,)), ((), ())), precision=HI,
                                                 preferred_element_type=jnp.float32)
    own = work[pl.ds(pl.multiple_of(x * 112, 8), 112), :]
    high = own.astype(jnp.bfloat16)
    rest = own - high.astype(jnp.float32)
    mid = rest.astype(jnp.bfloat16)
    low = (rest - mid.astype(jnp.float32)).astype(jnp.bfloat16)
    nt = (((1,), (1,)), ((), ()))
    acc = jnp.zeros((ROWS, 112), jnp.float32)
    for b in range(4):
        for piece in (low, mid, high):
            acc += lax.dot_general(proj[b][:, 0:112], piece[:, b * 112:(b + 1) * 112], nt,
                                   preferred_element_type=jnp.float32)
    out[...] = acc


def factor(gram, proj):
    vm = pl.BlockSpec(memory_space=pltpu.VMEM)
    return pl.pallas_call(
        factor_kernel,
        out_shape=[jax.ShapeDtypeStruct((448, 448), jnp.float32), jax.ShapeDtypeStruct((ROWS, 112), jnp.float32)],
        in_specs=[vm, vm],
        out_specs=[vm, vm],
        scratch_shapes=[pltpu.VMEM((448, 448), jnp.float32)],
        compiler_params=pltpu.CompilerParams(vmem_limit_bytes=40 * MIB),
        name="factor",
    )(gram, proj)


def shard_rows(block, core):
    rows = jnp.pad(block, ((0, 0), (0, 1), (0, 16))).reshape(7, 2, HALF).transpose(1, 0, 2)
    return jnp.where(core == 0, jnp.pad(rows, ((0, 0), (0, 9), (0, 0))), jnp.pad(rows, ((0, 0), (7, 2), (0, 0))))


def on_device(left_edge, corner, right_edge, single_layer, warm_basis):
    core = lax.axis_index("wide") % 2
    right = shard_rows(right_edge, core)
    warm = shard_rows(warm_basis.transpose(2, 0, 1), core)
    left = left_edge.reshape(7, 7, 7, 112).transpose(0, 2, 1, 3)
    left = jnp.pad(left, ((0, 0), (0, 0), (0, 1), (0, 16))).reshape(392, 128)
    left = jnp.pad(left, ((0, 8), (0, 0)))
    corner = jnp.pad(corner.reshape(112, 32, 14), ((0, 16), (0, 0), (0, 2))).reshape(128, 512)
    proj, gram = gathers(right, warm, left, corner, single_layer.reshape(2, 49, 49))
    r_factor, rows = factor(gram, proj)
    new_basis = rows[:392].reshape(7, 7, 8, 112)[:, :, :7].reshape(7, 49, 112)
    return new_basis, r_factor


def solution(mesh):
    placed = (
        P("wide", None, "narrow"),
        P("narrow", None),
        P("wide", None, "narrow"),
        P(),
        P(None, "narrow", "wide"),
    )
    return jax.shard_map(
        on_device,
        mesh=mesh,
        in_specs=placed,
        out_specs=(P("wide", None, "narrow"), P()),
        check_vma=False,
    )
```
